32 devices in a mesh: seg: 8 (over y, x, core), head: 4 (over z).
Axes of the slice: x: 2, y: 2, z: 4, core: 2. Of those that a mesh axis runs over, the one named last changes fastest.
Arguments:
- query_feat: float32 [1792, 25600], P('head', 'seg'), may hold values from -6 to 6
- key_feat: float32 [1792, 25600], P('head', 'seg'), may hold values from -6 to 6
- value_feat: float32 [1792, 25600], P('head', 'seg'), may hold values from -5.5 to 5.5
- grad_out: float32 [1792, 25600], P('head', 'seg'), may hold values from -6 to 6
- spatial_weight: float32 [3, 3, 1792], replicated, may hold values from -2 to 2
- temporal_weight: float32 [3, 1792], replicated, may hold values from -3.5 to 3.5
Outputs:
- grad_query: float32 [1792, 25600], P('head', 'seg')
- grad_key: float32 [1792, 25600], P('head', 'seg')
- grad_value: float32 [1792, 25600], P('head', 'seg')
- mixed: float32 [32, 20, 40, 1792], P('seg', None, 'head')
The draws below stay inside these ranges and needn't reach their ends.
All inputs are finite; a program needn't handle non-finite values.
Results may differ from the reference program's by a relative error of at most 0.00008.
Values sent between devices are 32-bit elements; how exact they have to be, the bound alone decides.
No kernel may reach another device: no remote copies, remote signals or barrier semaphores. Data moves between devices by JAX's collectives and lax.ppermute only.
A program may use at most 128 MiB of HBM per device.

```python
import jax
import jax.numpy as jnp
from jax import lax

HEAD_SIZE = 112
HEADS = 16
ROWS = 20
COLS = 40
FRAMES = 32
TOKENS = 25600
CHANNELS = 1792


def shared_base(key):
    shape = (HEADS * HEAD_SIZE, FRAMES * ROWS * COLS)
    base = jax.random.normal(jax.random.fold_in(key, 101), shape, jnp.float32)
    noise = jax.random.normal(jax.random.fold_in(key, 102), shape, jnp.float32)
    return (jnp.clip(base, -4.0, 4.0), jnp.clip(noise, -3.0, 3.0))


def draw_key_feat(key, part):
    base, noise = shared_base(key)
    return 1.5 * base


def draw_value_feat(key, part):
    base, noise = shared_base(key)
    return base + 0.5 * noise


def levels(rng, dims, pieces, least, high):
    def one(dim, parts):
        heights = jax.random.uniform(jax.random.fold_in(jax.random.fold_in(rng, 6), dim), (parts,), jnp.float32, least / len(pieces), high / len(pieces))
        return jnp.repeat(jnp.exp(heights), dims[dim] // parts).reshape((-1,) + (1,) * (len(dims) - dim - 1))

    factor_of = one(*pieces[0])
    for cut in pieces[1:]:
        factor_of = factor_of * one(*cut)
    return factor_of


def bell_draw(stream_key, shape, deviation, bound, split=(), dtype=jnp.bfloat16):
    drawn = deviation * jax.random.normal(stream_key, shape, jnp.float32)
    if split:
        drawn = drawn * levels(stream_key, shape, split, -0.22, 0.18)
    return jnp.clip(drawn, -bound, bound).astype(dtype)


def setup_inputs(seed: int = 0) -> dict:
    arg_keys = jax.random.split(jax.random.key(seed), 7)
    query_feat = bell_draw(arg_keys[0], (CHANNELS, TOKENS), 1.5, 6.0, ((0, 4), (1, 8)), jnp.float32)
    key_feat = draw_key_feat(jax.random.fold_in(arg_keys[6], 71), 0)
    value_feat = draw_value_feat(jax.random.fold_in(arg_keys[6], 71), 0)
    grad_out = bell_draw(arg_keys[3], (CHANNELS, TOKENS), 1.0, 6.0, ((0, 4), (1, 8)), jnp.float32)
    spatial_weight = bell_draw(arg_keys[4], (3, 3, CHANNELS), 9 ** -0.5, 2.0, (), jnp.float32)
    temporal_weight = bell_draw(arg_keys[5], (3, CHANNELS), 3 ** -0.5, 3.5, (), jnp.float32)
    return dict(query_feat=query_feat, key_feat=key_feat, value_feat=value_feat, grad_out=grad_out, spatial_weight=spatial_weight, temporal_weight=temporal_weight)


exact = lax.Precision.HIGHEST


def head_pass(inputs):
    query_h, key_h, value_h, grad_h = inputs
    feat_query = jnp.exp(query_h)
    feat_key = jnp.exp(key_h)
    local_kv = jnp.einsum('fpd,fpe->fde', feat_key, value_h, precision=exact)
    states = jnp.cumsum(local_kv, axis=0)
    key_sums = jnp.cumsum(jnp.sum(feat_key, axis=1), axis=0)
    numer = jnp.einsum('fpd,fde->fpe', feat_query, states, precision=exact)
    denom = jnp.einsum('fpd,fd->fp', feat_query, key_sums, precision=exact)
    attended = numer / denom[..., None]
    grad_numer = grad_h / denom[..., None]
    grad_denom = -jnp.sum(grad_h * attended, axis=-1) / denom
    grad_query = (jnp.einsum('fpe,fde->fpd', grad_numer, states, precision=exact) + grad_denom[..., None] * key_sums[:, None, :]) * feat_query
    grad_states = jnp.einsum('fpd,fpe->fde', feat_query, grad_numer, precision=exact)
    grad_sums = jnp.einsum('fpd,fp->fd', feat_query, grad_denom, precision=exact)
    later_states = jnp.flip(jnp.cumsum(jnp.flip(grad_states, 0), axis=0), 0)
    later_sums = jnp.flip(jnp.cumsum(jnp.flip(grad_sums, 0), axis=0), 0)
    grad_key = (jnp.einsum('fpe,fde->fpd', value_h, later_states, precision=exact) + later_sums[:, None, :]) * feat_key
    grad_value = jnp.einsum('fpd,fde->fpe', feat_key, later_states, precision=exact)
    return attended, grad_query, grad_key, grad_value


def to_heads(array):
    return jnp.transpose(array.reshape(HEADS, HEAD_SIZE, FRAMES, ROWS * COLS), (0, 2, 3, 1))


def from_heads(array):
    return jnp.transpose(array, (0, 3, 1, 2)).reshape(HEADS * HEAD_SIZE, FRAMES * ROWS * COLS)


def reference(query_feat, key_feat, value_feat, grad_out, spatial_weight, temporal_weight):
    results = lax.map(head_pass, (to_heads(query_feat), to_heads(key_feat), to_heads(value_feat), to_heads(grad_out)))
    attended_heads, grad_query, grad_key, grad_value = results
    attended = jnp.moveaxis(attended_heads, 0, 2).reshape(FRAMES, ROWS, COLS, HEADS * HEAD_SIZE)
    padded = jnp.pad(attended, ((0, 0), (1, 1), (1, 1), (0, 0)))
    spatial = jnp.zeros_like(attended)
    for row_off in range(3):
        for col_off in range(3):
            spatial = spatial + spatial_weight[row_off, col_off] * padded[:, row_off:row_off + ROWS, col_off:col_off + COLS]
    active = jax.nn.silu(spatial)
    past = jnp.pad(active, ((2, 0), (0, 0), (0, 0), (0, 0)))
    mixed = jnp.zeros_like(active)
    for lag in range(3):
        mixed = mixed + temporal_weight[lag] * past[2 - lag:2 - lag + FRAMES]
    return from_heads(grad_query), from_heads(grad_key), from_heads(grad_value), mixed
```

```python
import functools

import jax
import jax.numpy as jnp
from jax import lax
from jax.experimental import pallas as pl
from jax.experimental.pallas import tpu as pltpu
from jax.sharding import PartitionSpec as P

HEAD_SIZE = 112
ROWS = 20
COLS = 40
LANES = 128
AUG = -(-(HEAD_SIZE + 1) // LANES) * LANES
BLOCK = 4
VMEM = 56 * 1024 * 1024

f32 = jnp.float32
bf16 = jnp.bfloat16


def split(x):
    high = x.astype(bf16)
    return high, (x - high.astype(f32)).astype(bf16)


def dot(a, b, dims):
    return lax.dot_general(a, b, (dims, ((), ())), preferred_element_type=f32)


def stacked(x):
    high, low = split(x)
    return jnp.concatenate([high, low], axis=0)


def over_tokens(a, b):
    rows, cols = a.shape[0], b.shape[0]
    whole = dot(stacked(a), stacked(b), ((1,), (1,)))
    top, low = whole[:rows], whole[rows:, :cols]
    return top[:, :cols] + (top[:, cols:] + low)


def prepared(state):
    high, low = split(state)
    top = jnp.concatenate([high, high], axis=1)
    return jnp.concatenate([top, jnp.concatenate([low, jnp.zeros_like(low)], axis=1)], axis=0)


def times(pieces, x):
    high, low = split(x)
    spare = jnp.zeros((AUG - HEAD_SIZE, x.shape[1]), bf16)
    whole = dot(pieces, jnp.concatenate([high, spare, low, spare], axis=0), ((1,), (0,)))
    return whole[:HEAD_SIZE] + whole[HEAD_SIZE:]


def windows(frames, span, tokens):
    out = []
    for f in range(frames):
        first, last = f * span, (f + 1) * span
        low = first // LANES * LANES
        high = min(-(-last // LANES) * LANES, tokens)
        out.append((low, high, first, last))
    return out


def inside(window):
    low, high, first, last = window
    lane = lax.broadcasted_iota(jnp.int32, (1, high - low), 1) + low
    return (lane >= first) & (lane < last)


def cost(flops, data):
    return pl.CostEstimate(flops=1, bytes_accessed=1, transcendentals=0)


def params(count=1):
    return pltpu.CompilerParams(
        dimension_semantics=("arbitrary",) * count, vmem_limit_bytes=VMEM
    )


def states_kernel(wins, key_ref, value_ref, local_ref, total_ref):
    total = jnp.zeros((HEAD_SIZE, AUG), f32)
    for f, win in enumerate(wins):
        low, high, _, _ = win
        feat = jnp.where(inside(win), jnp.exp(key_ref[:, low:high]), 0.0)
        ones = jnp.ones((AUG - HEAD_SIZE, high - low), f32)
        value = jnp.concatenate([value_ref[:, low:high], ones], axis=0)
        part = over_tokens(feat, value)
        local_ref[0, f] = part
        total = total + part
    total_ref[0] = total


def local_states(key_feat, value_feat, frames, heads):
    tokens = key_feat.shape[1]
    wins = windows(frames, ROWS * COLS, tokens)
    block = pl.BlockSpec((HEAD_SIZE, tokens), lambda h: (h, 0))
    return pl.pallas_call(
        functools.partial(states_kernel, wins),
        grid=(heads,),
        in_specs=[block, block],
        out_specs=[
            pl.BlockSpec((1, frames, HEAD_SIZE, AUG), lambda h: (h, 0, 0, 0)),
            pl.BlockSpec((1, HEAD_SIZE, AUG), lambda h: (h, 0, 0)),
        ],
        out_shape=[
            jax.ShapeDtypeStruct((heads, frames, HEAD_SIZE, AUG), f32),
            jax.ShapeDtypeStruct((heads, HEAD_SIZE, AUG), f32),
        ],
        compiler_params=params(),
        cost_estimate=cost(6 * heads * tokens * AUG * AUG, 8 * heads * HEAD_SIZE * tokens),
        name="local_states",
    )(key_feat, value_feat)


def xor_move(array, axis, by):
    count = lax.axis_size(axis)
    return lax.ppermute(array, axis, [(i, i ^ by) for i in range(count)])


def joined_kernel(reverse, steps, *refs):
    blocks, out_ref = refs[: len(steps)], refs[-1]
    place = lax.axis_index("seg")
    total = jnp.zeros(out_ref.shape, f32)
    for by, block in zip(steps, blocks):
        ahead = (place ^ by) > place if reverse else (place ^ by) < place
        total = total + jnp.where(ahead, block[...], 0.0)
    out_ref[...] = total


def joined(reverse, steps, blocks, after):
    one = blocks[0]
    block = pl.BlockSpec(one.shape, lambda: (0,) * one.ndim)
    return pl.pallas_call(
        functools.partial(joined_kernel, reverse, steps),
        in_specs=[block] * len(blocks) + [pl.BlockSpec(memory_space=pl.ANY)] * len(after),
        out_specs=block,
        out_shape=jax.ShapeDtypeStruct(one.shape, f32),
        name="joined",
    )(*blocks, *after)


def entering(total, reverse, after):
    count = lax.axis_size("seg")
    odd = (lax.axis_index("seg") & 1) == 1
    half = total.shape[0] // 2
    mate = xor_move(total, "seg", 1)
    mine = jnp.where(odd, total[half:] + mate[half:], total[:half] + mate[:half])
    steps = tuple(range(2, count, 2))
    blocks = [xor_move(mine, "seg", by) for by in steps]
    part = joined(reverse, steps, blocks, after)
    return part, xor_move(part, "seg", 1), mate


def whole_state(parts, reverse):
    part, other, mate = parts
    odd = (lax.axis_index("seg") & 1) == 1
    full = jnp.where(
        odd, jnp.concatenate([other, part], axis=0), jnp.concatenate([part, other], axis=0)
    )
    late = jnp.logical_not(odd) if reverse else odd
    return full + jnp.where(late, mate, 0.0)


def turn_kernel(query_ref, out_ref):
    out_ref[...] = jnp.exp(query_ref[...]).T


def turned(query_feat):
    chans, tokens = query_feat.shape
    step = 640 if tokens % 640 == 0 else tokens
    return pl.pallas_call(
        turn_kernel,
        grid=(tokens // step,),
        in_specs=[pl.BlockSpec((chans, step), lambda i: (0, i))],
        out_specs=pl.BlockSpec((step, chans), lambda i: (i, 0)),
        out_shape=jax.ShapeDtypeStruct((tokens, chans), f32),
        compiler_params=params(),
        cost_estimate=cost(0, 8 * chans * tokens),
        name="turned",
    )(query_feat)


def forward_kernel(
    start, frames, heads, head_devs, part_ref, other_ref, mate_ref, local_ref, spatial_ref,
    temporal_ref, prev_ref, cur_ref, next_ref, *rest
):
    late_ref, early_ref, halo_ref, bd_high, bd_low, weight_ref = rest[-6:]
    chans = heads * HEAD_SIZE
    wide = bd_high.shape[2]
    width = COLS // head_devs
    half = BLOCK // 2
    step = pl.program_id(0)

    @pl.when(step == 0)
    def _():
        me = lax.axis_index("head")
        odd = (lax.axis_index("seg") & 1) == 1
        weight_ref[...] = jnp.zeros_like(weight_ref)
        for z in range(head_devs):

            @pl.when(me == z)
            def _():
                at = slice(z * chans, (z + 1) * chans)
                for r in range(3):
                    weight_ref[3 * r : 3 * r + 3, :chans] = spatial_ref[r, :, at]
                weight_ref[9:12, :chans] = temporal_ref[:, at]

        lane = lax.broadcasted_iota(jnp.int32, (HEAD_SIZE, LANES), 1)
        last = wide // LANES - 1
        for h in range(heads):
            first, second = part_ref, other_ref
            if h >= heads // 2:
                first, second = second, first
            g = h % (heads // 2)
            state = jnp.where(odd, second[g] + mate_ref[h], first[g])
            tile, shift = divmod(h * HEAD_SIZE, LANES)
            over = shift + HEAD_SIZE - LANES
            at = pl.ds(h * HEAD_SIZE, HEAD_SIZE)
            for f in range(frames):
                state = state + local_ref[h, f]
                moved = pltpu.roll(state, shift, 1) if shift else state
                sums = state[:, HEAD_SIZE : HEAD_SIZE + 1]
                for t in range(last + 1):
                    value = None
                    if t == tile:
                        value = jnp.where((lane >= shift) & (lane < shift + HEAD_SIZE), moved, 0.0)
                    elif t == tile + 1 and over > 0:
                        value = jnp.where(lane < over, moved, 0.0)
                    if t == last:
                        value = jnp.zeros_like(state) if value is None else value
                        value = jnp.where(lane == chans - last * LANES + h, sums, value)
                    span = slice(t * LANES, (t + 1) * LANES)
                    if value is None:
                        bd_high[f, at, span] = jnp.zeros((HEAD_SIZE, LANES), bf16)
                        bd_low[f, at, span] = jnp.zeros((HEAD_SIZE, LANES), bf16)
                    else:
                        bd_high[f, at, span], bd_low[f, at, span] = split(value)

    block = start + step
    top = jnp.where(block == 0, 0.0, 1.0)
    bottom = jnp.where(block == ROWS // BLOCK - 1, 0.0, 1.0)
    count = (BLOCK + 2) * COLS
    mids = BLOCK * COLS
    column = lax.broadcasted_iota(jnp.int32, (count, 1), 0) % COLS
    head_of = lax.broadcasted_iota(jnp.int32, (1, wide), 1) // HEAD_SIZE

    def active(f):
        feat = jnp.concatenate([prev_ref[f], cur_ref[f], next_ref[f]], axis=0)
        high, low = split(feat)
        numer = dot(high, bd_low[f], ((1,), (0,))) + dot(low, bd_high[f], ((1,), (0,)))
        numer = numer + dot(high, bd_high[f], ((1,), (0,)))
        inverse = 1.0 / numer[:, chans : chans + heads]
        scale = inverse[:, heads - 1 : heads]
        for h in range(heads - 2, -1, -1):
            scale = jnp.where(head_of <= h, inverse[:, h : h + 1], scale)
        att = numer * scale
        att = jnp.concatenate([att[:COLS] * top, att[COLS:-COLS], att[-COLS:] * bottom], axis=0)
        left = jnp.where(column == 0, 0.0, pltpu.roll(att, 1, 0))
        right = jnp.where(column == COLS - 1, 0.0, pltpu.roll(att, count - 1, 0))
        total = jnp.zeros((mids, wide), f32)
        for r in range(3):
            for c, side in enumerate((left, att, right)):
                total = total + weight_ref[3 * r + c : 3 * r + c + 1, :] * side[r * COLS : r * COLS + mids]
        return total / (1.0 + jnp.exp(-total))

    taps = [weight_ref[9 + i : 10 + i, :] for i in range(3)]
    acts = [active(f) for f in range(frames)]

    def put(ref, k, value):
        for z in range(head_devs):
            for r in range(BLOCK):
                rows = value[r * COLS + z * width : r * COLS + (z + 1) * width, :chans]
                ref[z, r % half, :, k, (r // half) * chans : (r // half + 1) * chans] = rows

    for f in range(2, frames):
        put(late_ref, f - 2, taps[0] * acts[f] + taps[1] * acts[f - 1] + taps[2] * acts[f - 2])
    put(early_ref, 0, taps[0] * acts[0])
    put(early_ref, 1, taps[0] * acts[1] + taps[1] * acts[0])
    put(halo_ref, 0, taps[1] * acts[-1] + taps[2] * acts[-2])
    put(halo_ref, 1, taps[2] * acts[-1])


def forward(parts, local, weights, feat, start, steps, head_devs, after):
    heads, frames = local.shape[:2]
    chans = heads * HEAD_SIZE
    wide = -(-(chans + heads) // LANES) * LANES
    parts = list(parts)
    width = COLS // head_devs
    half = BLOCK // 2
    last = ROWS // BLOCK

    def whole(a):
        return pl.BlockSpec(a.shape, lambda i: (0,) * a.ndim)

    def out(count):
        shape = (head_devs, steps * half, width, count, 2 * chans)
        spec = pl.BlockSpec((head_devs, half, width, count, 2 * chans), lambda i: (0, i, 0, 0, 0))
        return jax.ShapeDtypeStruct(shape, f32), spec

    outs = [out(frames - 2), out(2), out(2)]
    feat = feat.reshape(frames, ROWS * COLS, chans)
    return pl.pallas_call(
        functools.partial(forward_kernel, start, frames, heads, head_devs),
        grid=(steps,),
        in_specs=[
                *[whole(p) for p in parts],
                whole(local),
                *[whole(w) for w in weights],
                pl.BlockSpec(
                    (frames, COLS, chans),
                    lambda i: (0, jnp.maximum((start + i) * BLOCK - 1, 0), 0),
                ),
                pl.BlockSpec((frames, BLOCK * COLS, chans), lambda i: (0, start + i, 0)),
                pl.BlockSpec(
                    (frames, COLS, chans),
                    lambda i: (0, jnp.minimum((start + i + 1) * BLOCK, ROWS - 1), 0),
                ),
            ]
            + [pl.BlockSpec(memory_space=pl.ANY)] * len(after),
        out_specs=[spec for _, spec in outs],
        scratch_shapes=[
                pltpu.VMEM((frames, chans, wide), bf16),
                pltpu.VMEM((frames, chans, wide), bf16),
                pltpu.VMEM((16, wide), f32),
        ],
        out_shape=[shape for shape, _ in outs],
        compiler_params=params(),
        cost_estimate=cost(6 * steps * 960 * wide * wide, steps * 8000000),
        name="forward_rows",
    )(*parts, local, *weights, feat, feat, feat, *after)


def query_kernel(wins, query_ref, grad_ref, before_ref, local_ref, *rest):
    out_ref, part_ref, total_ref = rest[-3:]
    state = before_ref[0]
    total = jnp.zeros((HEAD_SIZE, AUG), f32)
    for f, win in enumerate(wins):
        low, high, _, _ = win
        keep = inside(win)
        state = state + local_ref[0, f]
        sums = state[:, HEAD_SIZE : HEAD_SIZE + 1]
        feat = jnp.exp(query_ref[:, low:high])
        inverse = 1.0 / jnp.sum(feat * sums, axis=0, keepdims=True)
        numer = grad_ref[:, low:high] * inverse
        moved = times(prepared(state), numer)
        denom = -jnp.sum(feat * moved, axis=0, keepdims=True) * inverse
        grad = (moved + sums * denom) * feat
        if low == 0:
            out_ref[:, low:high] = grad
        else:
            out_ref[:, low:high] = jnp.where(keep, grad, out_ref[:, low:high])
        spare = jnp.zeros((AUG - HEAD_SIZE - 8, high - low), f32)
        both = jnp.concatenate([numer, jnp.broadcast_to(denom, (8, high - low)), spare], axis=0)
        both = jnp.where(keep, both, 0.0)
        part = over_tokens(feat, both)
        part_ref[0, f] = part
        total = total + part
    total_ref[0] = total


def query_grads(query_feat, grad_out, before, local, after):
    tokens = query_feat.shape[1]
    heads, frames = local.shape[:2]
    wins = windows(frames, ROWS * COLS, tokens)
    block = pl.BlockSpec((HEAD_SIZE, tokens), lambda h: (h, 0))
    one = pl.BlockSpec((1, HEAD_SIZE, AUG), lambda h: (h, 0, 0))
    each = pl.BlockSpec((1, frames, HEAD_SIZE, AUG), lambda h: (h, 0, 0, 0))
    return pl.pallas_call(
        functools.partial(query_kernel, wins),
        grid=(heads,),
        in_specs=[block, block, one, each] + [pl.BlockSpec(memory_space=pl.ANY)] * len(after),
        out_specs=[block, each, one],
        out_shape=[
            jax.ShapeDtypeStruct(query_feat.shape, f32),
            jax.ShapeDtypeStruct(local.shape, f32),
            jax.ShapeDtypeStruct(before.shape, f32),
        ],
        compiler_params=params(),
        cost_estimate=cost(12 * heads * tokens * AUG * AUG, 12 * heads * HEAD_SIZE * tokens),
        name="query_grads",
    )(query_feat, grad_out, before, local, *after)


def key_kernel(wins, key_ref, value_ref, after_ref, part_ref, *rest):
    grad_key_ref, grad_value_ref = rest[-2:]
    state = after_ref[0]
    for f in range(len(wins) - 1, -1, -1):
        low, high, _, _ = wins[f]
        keep = inside(wins[f])
        state = state + part_ref[0, f]
        feat = jnp.exp(key_ref[:, low:high])
        value = value_ref[:, low:high]
        sums = state[:, HEAD_SIZE : HEAD_SIZE + 1]
        grad_key = (times(prepared(state), value) + sums) * feat
        turn = jnp.concatenate([state, jnp.zeros((AUG - HEAD_SIZE, AUG), f32)], axis=0).T
        grad_value = times(prepared(turn[:HEAD_SIZE]), feat)
        if f == len(wins) - 1:
            grad_key_ref[:, low:high] = grad_key
            grad_value_ref[:, low:high] = grad_value
        else:
            grad_key_ref[:, low:high] = jnp.where(keep, grad_key, grad_key_ref[:, low:high])
            grad_value_ref[:, low:high] = jnp.where(keep, grad_value, grad_value_ref[:, low:high])


def key_grads(key_feat, value_feat, later, part, after):
    tokens = key_feat.shape[1]
    heads, frames = part.shape[:2]
    wins = windows(frames, ROWS * COLS, tokens)
    block = pl.BlockSpec((HEAD_SIZE, tokens), lambda h: (h, 0))
    return pl.pallas_call(
        functools.partial(key_kernel, wins),
        grid=(heads,),
        in_specs=[
            block,
            block,
            pl.BlockSpec((1, HEAD_SIZE, AUG), lambda h: (h, 0, 0)),
            pl.BlockSpec((1, frames, HEAD_SIZE, AUG), lambda h: (h, 0, 0, 0)),
        ]
        + [pl.BlockSpec(memory_space=pl.ANY)] * len(after),
        out_specs=[block, block],
        out_shape=[jax.ShapeDtypeStruct(key_feat.shape, f32)] * 2,
        compiler_params=params(),
        cost_estimate=cost(12 * heads * tokens * AUG * AUG, 16 * heads * HEAD_SIZE * tokens),
        name="key_grads",
    )(key_feat, value_feat, later, part, *after)


def topped_kernel(early_ref, halo_ref, *rest):
    rest[-1][...] = early_ref[...] + halo_ref[...]


def topped(early, halo, after):
    block = pl.BlockSpec((1, *early.shape[1:]), lambda z: (z, 0, 0, 0, 0))
    return pl.pallas_call(
        topped_kernel,
        grid=(early.shape[0],),
        in_specs=[block, block] + [pl.BlockSpec(memory_space=pl.ANY)] * len(after),
        out_specs=block,
        out_shape=jax.ShapeDtypeStruct(early.shape, f32),
        compiler_params=params(),
        cost_estimate=cost(0, 0),
        name="topped",
    )(early, halo, *after)


def place_kernel(chans, early_ref, late_ref, *rest):
    out_ref = rest[-1]
    half = BLOCK // 2
    for first, ref in ((0, early_ref), (2, late_ref)):
        for r in range(half):
            for j in range(ref.shape[0]):
                value = ref[j, r]
                for side in range(2):
                    out_ref[
                        r + side * half, :, first : first + value.shape[1], j * chans : (j + 1) * chans
                    ] = value[:, :, side * chans : (side + 1) * chans]


def placed(early, late, filled, start, steps, chans):
    half = BLOCK // 2
    width = early.shape[2]
    frames = early.shape[3] + late.shape[3]
    total = early.shape[0] * chans

    def spec(a):
        return pl.BlockSpec((a.shape[0], half, *a.shape[2:]), lambda i: (0, i, 0, 0, 0))

    extra = [] if filled is None else [filled]
    return pl.pallas_call(
        functools.partial(place_kernel, chans),
        grid=(steps,),
        in_specs=[spec(early), spec(late)] + [pl.BlockSpec(memory_space=pl.ANY)] * len(extra),
        out_specs=pl.BlockSpec((BLOCK, width, frames, total), lambda i: (start + i, 0, 0, 0)),
        out_shape=jax.ShapeDtypeStruct((ROWS, width, frames, total), f32),
        input_output_aliases={2: 0} if extra else {},
        compiler_params=params(),
        cost_estimate=cost(0, steps * 2400000),
        name="placed",
    )(early, late, *extra)


def body(query_feat, key_feat, value_feat, grad_out, spatial_weight, temporal_weight):
    chans, tokens = query_feat.shape
    frames = tokens // (ROWS * COLS)
    heads = chans // HEAD_SIZE
    head_devs = lax.axis_size("head")
    segs = lax.axis_size("seg")
    local, totals = local_states(key_feat, value_feat, frames, heads)
    feat = turned(query_feat)
    parts = entering(totals, False, [feat])

    def sent(a):
        return lax.all_to_all(a, "head", split_axis=0, concat_axis=0, tiled=True)

    spans = [(0, 1), (1, ROWS // BLOCK - 1)]
    late, early, halo = [], [], []
    after = []
    for start, steps in spans:
        a, b, c = forward(parts, local, (spatial_weight, temporal_weight), feat, start, steps, head_devs, after)
        late.append(sent(a))
        early.append(b)
        halo.append(c)
        after = [c]
    pairs = [(i, i + 1) for i in range(segs - 1)]
    moved = [lax.ppermute(c, "seg", pairs) for c in halo]

    before = whole_state(parts, False)
    grad_query, part, back = query_grads(query_feat, grad_out, before, local, [late[0], halo[-1]])
    later = whole_state(entering(back, True, []), True)
    grad_key, grad_value = key_grads(key_feat, value_feat, later, part, [])

    last = sent(topped(early[1], moved[1], [grad_key]))
    first = sent(topped(early[0], moved[0], [late[1]]))
    mixed = placed(last, late[1], None, *spans[1], chans)
    mixed = placed(first, late[0], mixed, *spans[0], chans)
    return grad_query, grad_key, grad_value, jnp.transpose(mixed, (2, 0, 1, 3))


def solution(mesh):
    in_specs = (P("head", "seg"), P("head", "seg"), P("head", "seg"), P("head", "seg"), P(), P())
    out_specs = (P("head", "seg"), P("head", "seg"), P("head", "seg"), P("seg", None, "head", None))
    return jax.shard_map(body, mesh=mesh, in_specs=in_specs, out_specs=out_specs, check_vma=False)
```

```python
import functools

import jax
import jax.numpy as jnp
from jax import lax
from jax.experimental import pallas as pl
from jax.experimental.pallas import tpu as pltpu
from jax.sharding import PartitionSpec as P

HEAD_SIZE = 112
ROWS = 20
COLS = 40
LANES = 128
AUG = -(-(HEAD_SIZE + 1) // LANES) * LANES
BLOCK = 4

f32 = jnp.float32
bf16 = jnp.bfloat16


def split(x):
    high = x.astype(bf16)
    return high, (x - high.astype(f32)).astype(bf16)


def dot(a, b, dims):
    return lax.dot_general(a, b, (dims, ((), ())), preferred_element_type=f32)


def stacked(x):
    high, low = split(x)
    return jnp.concatenate([high, low], axis=0)


def over_tokens(a, b):
    rows, cols = a.shape[0], b.shape[0]
    whole = dot(stacked(a), stacked(b), ((1,), (1,)))
    top, low = whole[:rows], whole[rows:, :cols]
    return top[:, :cols] + (top[:, cols:] + low)


def prepared(state):
    high, low = split(state)
    top = jnp.concatenate([high, high], axis=1)
    return jnp.concatenate([top, jnp.concatenate([low, jnp.zeros_like(low)], axis=1)], axis=0)


def times(pieces, x):
    high, low = split(x)
    spare = jnp.zeros((AUG - HEAD_SIZE, x.shape[1]), bf16)
    whole = dot(pieces, jnp.concatenate([high, spare, low, spare], axis=0), ((1,), (0,)))
    return whole[:HEAD_SIZE] + whole[HEAD_SIZE:]


def windows(frames, span, tokens):
    out = []
    for f in range(frames):
        first, last = f * span, (f + 1) * span
        low = first // LANES * LANES
        high = min(-(-last // LANES) * LANES, tokens)
        out.append((low, high, first, last))
    return out


def inside(window):
    low, high, first, last = window
    lane = lax.broadcasted_iota(jnp.int32, (1, high - low), 1) + low
    return (lane >= first) & (lane < last)


def in_hbm(shape):
    return pltpu.HBM(shape, f32)


def cost(flops, data):
    return pl.CostEstimate(flops=1, bytes_accessed=1, transcendentals=0)


def params(mib):
    return pltpu.CompilerParams(
        dimension_semantics=("arbitrary",), vmem_limit_bytes=mib * 1024 * 1024
    )


def states_kernel(wins, heads, key_any, value_any, local_ref, total_ref, key_buf, value_buf, sems):
    middle = wins[(len(wins) - 1) // 2][1]
    halves = (slice(0, middle), slice(middle, wins[-1][1]))

    def copies(h, half):
        at = pl.ds(h * HEAD_SIZE, HEAD_SIZE)
        pairs = ((key_any, key_buf), (value_any, value_buf))
        return [
            pltpu.make_async_copy(
                src.at[at, halves[half]], dst.at[h, :, halves[half]], sems.at[i, half, h]
            )
            for i, (src, dst) in enumerate(pairs)
        ]

    halved = 2 if middle < wins[-1][1] else 1
    for h in range(heads):
        for half in range(halved):
            for copy in copies(h, half):
                copy.start()
    for h in range(heads):
        total = jnp.zeros((HEAD_SIZE, AUG), f32)
        for f, win in enumerate(wins):
            for half in range(halved):
                if f == (0, (len(wins) - 1) // 2 + 1)[half]:
                    for copy in copies(h, half):
                        copy.wait()
            low, high, _, _ = win
            feat = jnp.where(inside(win), jnp.exp(key_buf[h, :, low:high]), 0.0)
            ones = jnp.ones((AUG - HEAD_SIZE, high - low), f32)
            value = jnp.concatenate([value_buf[h, :, low:high], ones], axis=0)
            part = over_tokens(feat, value)
            local_ref[h, f] = part
            total = total + part
        total_ref[h] = total


def local_states(key_feat, value_feat, frames, heads):
    tokens = key_feat.shape[1]
    wins = windows(frames, ROWS * COLS, tokens)
    return pl.pallas_call(
        functools.partial(states_kernel, wins, heads),
        in_specs=[pl.BlockSpec(memory_space=pltpu.HBM)] * 2,
        out_shape=[
            jax.ShapeDtypeStruct((heads, frames, HEAD_SIZE, AUG), f32),
            jax.ShapeDtypeStruct((heads, HEAD_SIZE, AUG), f32),
        ],
        scratch_shapes=[
            pltpu.VMEM((heads, HEAD_SIZE, tokens), f32),
            pltpu.VMEM((heads, HEAD_SIZE, tokens), f32),
            pltpu.SemaphoreType.DMA((2, 2, heads)),
        ],
        compiler_params=pltpu.CompilerParams(vmem_limit_bytes=56 * 1024 * 1024),
        cost_estimate=cost(0, 0),
        name="local_states",
    )(key_feat, value_feat)


def xor_move(array, axis, by):
    count = lax.axis_size(axis)
    return lax.ppermute(array, axis, [(i, i ^ by) for i in range(count)])


def joined_kernel(reverse, steps, *refs):
    blocks, out_ref = refs[: len(steps)], refs[-1]
    place = lax.axis_index("seg")
    total = jnp.zeros(out_ref.shape, f32)
    for by, block in zip(steps, blocks):
        ahead = (place ^ by) > place if reverse else (place ^ by) < place
        total = total + jnp.where(ahead, block[...], 0.0)
    out_ref[...] = total


def joined(reverse, steps, blocks, after):
    one = blocks[0]
    block = pl.BlockSpec(one.shape, lambda: (0,) * one.ndim)
    return pl.pallas_call(
        functools.partial(joined_kernel, reverse, steps),
        in_specs=[block] * len(blocks) + [pl.BlockSpec(memory_space=pltpu.HBM)] * len(after),
        out_specs=block,
        out_shape=jax.ShapeDtypeStruct(one.shape, f32),
        compiler_params=pltpu.CompilerParams(vmem_limit_bytes=8 * 1024 * 1024),
        name="joined",
    )(*blocks, *after)


def entering(total, reverse, after):
    count = lax.axis_size("seg")
    odd = (lax.axis_index("seg") & 1) == 1
    half = total.shape[0] // 2
    mate = xor_move(total, "seg", 1)
    mine = jnp.where(odd, total[half:] + mate[half:], total[:half] + mate[:half])
    steps = tuple(range(2, count, 2))
    blocks = [xor_move(mine, "seg", by) for by in steps]
    part = joined(reverse, steps, blocks, after)
    return part, xor_move(part, "seg", 1), mate


def whole_state(parts, reverse):
    part, other, mate = parts
    odd = (lax.axis_index("seg") & 1) == 1
    full = jnp.where(
        odd, jnp.concatenate([other, part], axis=0), jnp.concatenate([part, other], axis=0)
    )
    late = jnp.logical_not(odd) if reverse else odd
    return full + jnp.where(late, mate, 0.0)


def turn_kernel(query_ref, out_ref):
    chans = query_ref.shape[0]
    out_ref[:, :chans] = jnp.exp(query_ref[...]).T
    out_ref[:, chans:] = jnp.zeros((out_ref.shape[0], out_ref.shape[1] - chans), f32)


def padded(chans):
    return -(-(chans + chans // HEAD_SIZE) // LANES) * LANES


def turned(query_feat):
    chans, tokens = query_feat.shape
    wide = padded(chans)
    step = 640 if tokens % 640 == 0 else tokens
    return pl.pallas_call(
        turn_kernel,
        grid=(tokens // step,),
        in_specs=[pl.BlockSpec((chans, step), lambda i: (0, i))],
        out_specs=pl.BlockSpec((step, wide), lambda i: (i, 0)),
        out_shape=jax.ShapeDtypeStruct((tokens, wide), f32),
        compiler_params=params(24),
        cost_estimate=cost(0, 0),
        name="turned",
    )(query_feat)


def forward_kernel(
    start, frames, heads, head_devs, part_ref, other_ref, mate_ref, local_ref, spatial_ref,
    temporal_ref, prev_ref, cur_ref, next_ref, *rest
):
    late_ref, early_ref, halo_ref, mix_ref, weight_ref, att_ref = rest[-6:]
    chans = heads * HEAD_SIZE
    wide = weight_ref.shape[1]
    width = COLS // head_devs
    step = pl.program_id(0)

    @pl.when(step == 0)
    def _():
        me = lax.axis_index("head")
        odd = (lax.axis_index("seg") & 1) == 1
        weight_ref[...] = jnp.zeros_like(weight_ref)
        for z in range(head_devs):

            @pl.when(me == z)
            def _():
                at = slice(z * chans, (z + 1) * chans)
                for r in range(3):
                    weight_ref[3 * r : 3 * r + 3, :chans] = spatial_ref[r, :, at]
                weight_ref[9:12, :chans] = temporal_ref[:, at]

        for f in range(frames):
            for k in range(3):
                spare = pl.ds(k * wide + chans, wide - chans)
                mix_ref[f, spare, :] = jnp.zeros((wide - chans, wide), bf16)
        lane = lax.broadcasted_iota(jnp.int32, (HEAD_SIZE, LANES), 1)
        last = wide // LANES - 1
        for h in range(heads):
            first, second = part_ref, other_ref
            if h >= heads // 2:
                first, second = second, first
            g = h % (heads // 2)
            state = jnp.where(odd, second[g] + mate_ref[h], first[g])
            tile, shift = divmod(h * HEAD_SIZE, LANES)
            over = shift + HEAD_SIZE - LANES
            at = [pl.ds(k * wide + h * HEAD_SIZE, HEAD_SIZE) for k in range(3)]
            for f in range(frames):
                state = state + local_ref[h, f]
                moved = pltpu.roll(state, shift, 1) if shift else state
                sums = state[:, HEAD_SIZE : HEAD_SIZE + 1]
                for t in range(last + 1):
                    value = None
                    if t == tile:
                        value = jnp.where((lane >= shift) & (lane < shift + HEAD_SIZE), moved, 0.0)
                    elif t == tile + 1 and over > 0:
                        value = jnp.where(lane < over, moved, 0.0)
                    if t == last:
                        value = jnp.zeros_like(state) if value is None else value
                        value = jnp.where(lane == chans - last * LANES + h, sums, value)
                    span = slice(t * LANES, (t + 1) * LANES)
                    if value is None:
                        high = low = jnp.zeros((HEAD_SIZE, LANES), bf16)
                    else:
                        high, low = split(value)
                    mix_ref[f, at[0], span] = low
                    mix_ref[f, at[1], span] = high
                    mix_ref[f, at[2], span] = high

    block = start + step
    top = jnp.where(block == 0, 0.0, 1.0)
    bottom = jnp.where(block == ROWS // BLOCK - 1, 0.0, 1.0)
    count = (BLOCK + 2) * COLS
    lane = lax.broadcasted_iota(jnp.int32, (1, LANES), 1)
    for f in range(frames):
        high, low = split(jnp.concatenate([prev_ref[f], cur_ref[f], next_ref[f]], axis=0))
        pieces = jnp.concatenate([high, low, high], axis=1)
        numer = dot(pieces, mix_ref[f], ((1,), (0,)))
        inverse = 1.0 / numer[:, chans : chans + heads]
        for t in range(wide // LANES):
            first = t * LANES // HEAD_SIZE
            final = min(((t + 1) * LANES - 1) // HEAD_SIZE, heads - 1)
            scale = inverse[:, final : final + 1]
            for h in range(final - 1, first - 1, -1):
                scale = jnp.where(lane < (h + 1) * HEAD_SIZE - t * LANES, inverse[:, h : h + 1], scale)
            span = slice(t * LANES, (t + 1) * LANES)
            att = numer[:, span] * scale
            att_ref[f, :COLS, span] = att[:COLS] * top
            att_ref[f, COLS : count - COLS, span] = att[COLS:-COLS]
            att_ref[f, count - COLS :, span] = att[-COLS:] * bottom

    column = lax.broadcasted_iota(jnp.int32, (COLS, 1), 0)
    for t in range(-(-chans // LANES)):
        span = slice(t * LANES, (t + 1) * LANES)
        used = min(LANES, chans - t * LANES)
        taps = [weight_ref[9 + i : 10 + i, span] for i in range(3)]
        for r in range(BLOCK):
            act = []
            for f in range(frames):
                rows = [att_ref[f, (r + k) * COLS : (r + k + 1) * COLS, span] for k in range(3)]
                sides = []
                for c in range(3):
                    weight = [weight_ref[3 * k + c : 3 * k + c + 1, span] for k in range(3)]
                    sides.append(weight[0] * rows[0] + weight[1] * rows[1] + weight[2] * rows[2])
                left = jnp.where(column == 0, 0.0, pltpu.roll(sides[0], 1, 0))
                right = jnp.where(column == COLS - 1, 0.0, pltpu.roll(sides[2], COLS - 1, 0))
                total = sides[1] + (left + right)
                act.append(total / (1.0 + jnp.exp(-total)))
            late = [taps[0] * act[f] + taps[1] * act[f - 1] + taps[2] * act[f - 2] for f in range(2, frames)]
            early = [taps[0] * act[0], taps[0] * act[1] + taps[1] * act[0]]
            halo = [taps[1] * act[-1] + taps[2] * act[-2], taps[2] * act[-1]]
            for ref, values in ((late_ref, late), (early_ref, early), (halo_ref, halo)):
                for k, value in enumerate(values):
                    low = k * chans + t * LANES
                    for z in range(head_devs):
                        ref[z, 0, r * width : (r + 1) * width, low : low + used] = value[
                            z * width : (z + 1) * width, :used
                        ]


def forward(parts, local, weights, feat, start, steps, head_devs, after):
    heads, frames = local.shape[:2]
    chans = heads * HEAD_SIZE
    wide = padded(chans)
    parts = list(parts)
    width = COLS // head_devs
    def whole(a):
        return pl.BlockSpec(a.shape, lambda i: (0,) * a.ndim)

    def out(count):
        shape = (head_devs, steps, BLOCK * width, count * chans)
        spec = pl.BlockSpec((head_devs, 1, *shape[2:]), lambda i: (0, i, 0, 0))
        return in_hbm(shape), spec

    outs = [out(frames - 2), out(2), out(2)]
    feat = feat.reshape(frames, ROWS * COLS, wide)
    return pl.pallas_call(
        functools.partial(forward_kernel, start, frames, heads, head_devs),
        grid=(steps,),
        in_specs=[
                *[whole(p) for p in parts],
                whole(local),
                *[whole(w) for w in weights],
                pl.BlockSpec(
                    (frames, COLS, wide),
                    lambda i: (0, jnp.maximum((start + i) * BLOCK - 1, 0), 0),
                ),
                pl.BlockSpec((frames, BLOCK * COLS, wide), lambda i: (0, start + i, 0)),
                pl.BlockSpec(
                    (frames, COLS, wide),
                    lambda i: (0, jnp.minimum((start + i + 1) * BLOCK, ROWS - 1), 0),
                ),
            ]
            + [pl.BlockSpec(memory_space=pltpu.HBM)] * len(after),
        out_specs=[spec for _, spec in outs],
        scratch_shapes=[
                pltpu.VMEM((frames, 3 * wide, wide), bf16),
                pltpu.VMEM((16, wide), f32),
                pltpu.VMEM((frames, (BLOCK + 2) * COLS, wide), f32),
        ],
        out_shape=[shape for shape, _ in outs],
        compiler_params=params(28 if steps == 1 else 58),
        cost_estimate=cost(6 * steps * 960 * wide * wide, steps * 8000000),
        name="forward_rows",
    )(*parts, local, *weights, feat, feat, feat, *after)


def query_kernel(wins, query_ref, grad_ref, before_ref, local_ref, *rest):
    out_ref, part_ref, total_ref = rest[-3:]
    state = before_ref[0]
    total = jnp.zeros((HEAD_SIZE, AUG), f32)
    for f, win in enumerate(wins):
        low, high, _, _ = win
        keep = inside(win)
        state = state + local_ref[0, f]
        sums = state[:, HEAD_SIZE : HEAD_SIZE + 1]
        feat = jnp.exp(query_ref[:, low:high])
        inverse = 1.0 / jnp.sum(feat * sums, axis=0, keepdims=True)
        numer = grad_ref[:, low:high] * inverse
        moved = times(prepared(state), numer)
        denom = -jnp.sum(feat * moved, axis=0, keepdims=True) * inverse
        grad = (moved + sums * denom) * feat
        if low == 0:
            out_ref[:, low:high] = grad
        else:
            out_ref[:, low:high] = jnp.where(keep, grad, out_ref[:, low:high])
        spare = jnp.zeros((AUG - HEAD_SIZE - 8, high - low), f32)
        both = jnp.concatenate([numer, jnp.broadcast_to(denom, (8, high - low)), spare], axis=0)
        both = jnp.where(keep, both, 0.0)
        part = over_tokens(feat, both)
        part_ref[0, f] = part
        total = total + part
    total_ref[0] = total


def query_grads(query_feat, grad_out, before, local, after):
    tokens = query_feat.shape[1]
    heads, frames = local.shape[:2]
    wins = windows(frames, ROWS * COLS, tokens)
    block = pl.BlockSpec((HEAD_SIZE, tokens), lambda h: (h, 0))
    one = pl.BlockSpec((1, HEAD_SIZE, AUG), lambda h: (h, 0, 0))
    each = pl.BlockSpec((1, frames, HEAD_SIZE, AUG), lambda h: (h, 0, 0, 0))
    return pl.pallas_call(
        functools.partial(query_kernel, wins),
        grid=(heads,),
        in_specs=[block, block, one, each] + [pl.BlockSpec(memory_space=pltpu.HBM)] * len(after),
        out_specs=[block, each, one],
        out_shape=[
            in_hbm(query_feat.shape),
            jax.ShapeDtypeStruct(local.shape, f32),
            jax.ShapeDtypeStruct(before.shape, f32),
        ],
        compiler_params=params(58),
        cost_estimate=cost(12 * heads * tokens * AUG * AUG, 12 * heads * HEAD_SIZE * tokens),
        name="query_grads",
    )(query_feat, grad_out, before, local, *after)


def key_kernel(wins, key_ref, value_ref, after_ref, part_ref, *rest):
    grad_key_ref, grad_value_ref = rest[-2:]
    state = after_ref[0]
    for f in range(len(wins) - 1, -1, -1):
        low, high, _, _ = wins[f]
        keep = inside(wins[f])
        state = state + part_ref[0, f]
        feat = jnp.exp(key_ref[:, low:high])
        value = value_ref[:, low:high]
        sums = state[:, HEAD_SIZE : HEAD_SIZE + 1]
        grad_key = (times(prepared(state), value) + sums) * feat
        turn = jnp.concatenate([state, jnp.zeros((AUG - HEAD_SIZE, AUG), f32)], axis=0).T
        grad_value = times(prepared(turn[:HEAD_SIZE]), feat)
        if f == len(wins) - 1:
            grad_key_ref[:, low:high] = grad_key
            grad_value_ref[:, low:high] = grad_value
        else:
            grad_key_ref[:, low:high] = jnp.where(keep, grad_key, grad_key_ref[:, low:high])
            grad_value_ref[:, low:high] = jnp.where(keep, grad_value, grad_value_ref[:, low:high])


def key_grads(key_feat, value_feat, later, part, after):
    tokens = key_feat.shape[1]
    heads, frames = part.shape[:2]
    wins = windows(frames, ROWS * COLS, tokens)
    block = pl.BlockSpec((HEAD_SIZE, tokens), lambda h: (h, 0))
    return pl.pallas_call(
        functools.partial(key_kernel, wins),
        grid=(heads,),
        in_specs=[
            block,
            block,
            pl.BlockSpec((1, HEAD_SIZE, AUG), lambda h: (h, 0, 0)),
            pl.BlockSpec((1, frames, HEAD_SIZE, AUG), lambda h: (h, 0, 0, 0)),
        ]
        + [pl.BlockSpec(memory_space=pltpu.HBM)] * len(after),
        out_specs=[block, block],
        out_shape=[in_hbm(key_feat.shape)] * 2,
        compiler_params=params(58),
        cost_estimate=cost(12 * heads * tokens * AUG * AUG, 16 * heads * HEAD_SIZE * tokens),
        name="key_grads",
    )(key_feat, value_feat, later, part, *after)


def topped_kernel(count, me_ref, *refs):
    for early_ref, halo_ref, out_ref in zip(refs, refs[count : 2 * count], refs[-count:]):
        out_ref[...] = early_ref[0] + halo_ref[0]


def topped(early, halo, after):
    count, steps = early.shape[:2]
    me = lax.axis_index("head").astype(jnp.int32).reshape(1)

    def block(s):
        return pl.BlockSpec((1, 1, *early.shape[2:]), lambda i, me: (me[0] ^ s, i, 0, 0))

    return pl.pallas_call(
        functools.partial(topped_kernel, count),
        grid_spec=pltpu.PrefetchScalarGridSpec(
            num_scalar_prefetch=1,
            grid=(steps,),
            in_specs=[block(s) for s in range(count)] * 2
            + [pl.BlockSpec(memory_space=pltpu.HBM)] * len(after),
            out_specs=[pl.BlockSpec((1, *early.shape[2:]), lambda i, me: (i, 0, 0))] * count,
        ),
        out_shape=[in_hbm(early.shape[1:])] * count,
        compiler_params=params(58),
        cost_estimate=cost(0, 0),
        name="topped",
    )(me, *[early] * count, *[halo] * count, *after)


def place_kernel(chans, count, *refs):
    late_ref, out_ref = refs[count], refs[-1]
    me = lax.axis_index("head")
    found = [ref[0] for ref in refs[:count]]
    bit = 1
    while bit < count:
        swap = (me & bit) != 0
        found = [jnp.where(swap, found[s ^ bit], found[s]) for s in range(count)]
        bit *= 2
    first = 0
    for blocks in (found, [late_ref[j, 0] for j in range(count)]):
        for k in range(blocks[0].shape[1] // chans):
            pieces = [block[:, k * chans : (k + 1) * chans] for block in blocks]
            out_ref[:, first, :] = jnp.concatenate(pieces, axis=1)
            first += 1


def placed(early, late, filled, start, steps, chans):
    count = len(early)
    rows = late.shape[2]
    frames = (early[0].shape[2] + late.shape[3]) // chans
    total = count * chans
    extra = [] if filled is None else [filled]
    return pl.pallas_call(
        functools.partial(place_kernel, chans, count),
        grid=(steps,),
        in_specs=[pl.BlockSpec((1, *a.shape[1:]), lambda i: (i, 0, 0)) for a in early]
        + [pl.BlockSpec((count, 1, *late.shape[2:]), lambda i: (0, i, 0, 0))]
        + [pl.BlockSpec(memory_space=pl.ANY)] * len(extra),
        out_specs=pl.BlockSpec((rows, frames, total), lambda i: (start + i, 0, 0)),
        out_shape=jax.ShapeDtypeStruct((rows * (ROWS // BLOCK), frames, total), f32),
        input_output_aliases={count + 1: 0} if extra else {},
        compiler_params=params(28),
        cost_estimate=cost(0, steps * 2400000),
        name="placed",
    )(*early, late, *extra)


def body(query_feat, key_feat, value_feat, grad_out, spatial_weight, temporal_weight):
    chans, tokens = query_feat.shape
    frames = tokens // (ROWS * COLS)
    heads = chans // HEAD_SIZE
    head_devs = lax.axis_size("head")
    segs = lax.axis_size("seg")
    local, totals = local_states(key_feat, value_feat, frames, heads)
    feat = turned(query_feat)
    parts = entering(totals, False, [feat])

    def sent(a):
        return lax.all_to_all(a, "head", split_axis=0, concat_axis=0, tiled=True)

    spans = [(0, 1), (1, ROWS // BLOCK - 1)]
    late, early, halo = [], [], []
    after = []
    for start, steps in spans:
        a, b, c = forward(parts, local, (spatial_weight, temporal_weight), feat, start, steps, head_devs, after)
        late.append(sent(a))
        early.append(b)
        halo.append(c)
        after = [c]
    pairs = [(i, i + 1) for i in range(segs - 1)]
    moved = [lax.ppermute(c, "seg", pairs) for c in halo]

    before = whole_state(parts, False)
    grad_query, part, back = query_grads(query_feat, grad_out, before, local, [late[0], halo[-1]])
    later = whole_state(entering(back, True, []), True)
    grad_key, grad_value = key_grads(key_feat, value_feat, later, part, [])

    def exchanged(blocks):
        return [blocks[0]] + [xor_move(a, "head", s) for s, a in enumerate(blocks) if s]

    last = exchanged(topped(early[1], moved[1], [grad_query]))
    first = exchanged(topped(early[0], moved[0], [grad_key]))
    mixed = placed(last, late[1], None, *spans[1], chans)
    mixed = placed(first, late[0], mixed, *spans[0], chans)
    mixed = mixed.reshape(ROWS, COLS // head_devs, *mixed.shape[1:])
    return grad_query, grad_key, grad_value, jnp.transpose(mixed, (2, 0, 1, 3))


def solution(mesh):
    in_specs = (P("head", "seg"), P("head", "seg"), P("head", "seg"), P("head", "seg"), P(), P())
    out_specs = (P("head", "seg"), P("head", "seg"), P("head", "seg"), P("seg", None, "head", None))
    return jax.shard_map(body, mesh=mesh, in_specs=in_specs, out_specs=out_specs, check_vma=False)
```

```python
import functools

import jax
import jax.numpy as jnp
from jax import lax
from jax.experimental import pallas as pl
from jax.experimental.pallas import tpu as pltpu
from jax.sharding import PartitionSpec as P

HEAD_SIZE = 112
ROWS = 20
COLS = 40
LANES = 128
AUG = -(-(HEAD_SIZE + 1) // LANES) * LANES
BLOCK = 4

f32 = jnp.float32
bf16 = jnp.bfloat16


def split(x):
    high = x.astype(bf16)
    return high, (x - high.astype(f32)).astype(bf16)


def dot(a, b, dims):
    return lax.dot_general(a, b, (dims, ((), ())), preferred_element_type=f32)


def stacked(x):
    high, low = split(x)
    return jnp.concatenate([high, low], axis=0)


def over_tokens(a, b):
    rows, cols = a.shape[0], b.shape[0]
    whole = dot(stacked(a), stacked(b), ((1,), (1,)))
    top, low = whole[:rows], whole[rows:, :cols]
    return top[:, :cols] + (top[:, cols:] + low)


def prepared(state):
    high, low = split(state)
    top = jnp.concatenate([high, high], axis=1)
    return jnp.concatenate([top, jnp.concatenate([low, jnp.zeros_like(low)], axis=1)], axis=0)


def times(pieces, x):
    high, low = split(x)
    spare = jnp.zeros((AUG - HEAD_SIZE, x.shape[1]), bf16)
    whole = dot(pieces, jnp.concatenate([high, spare, low, spare], axis=0), ((1,), (0,)))
    return whole[:HEAD_SIZE] + whole[HEAD_SIZE:]


def windows(frames, span, tokens):
    out = []
    for f in range(frames):
        first, last = f * span, (f + 1) * span
        low = first // LANES * LANES
        high = min(-(-last // LANES) * LANES, tokens)
        out.append((low, high, first, last))
    return out


def inside(window):
    low, high, first, last = window
    lane = lax.broadcasted_iota(jnp.int32, (1, high - low), 1) + low
    return (lane >= first) & (lane < last)


def in_hbm(shape):
    return pltpu.HBM(shape, f32)


def cost(flops, data):
    return pl.CostEstimate(flops=1, bytes_accessed=1, transcendentals=0)


def params(mib):
    return pltpu.CompilerParams(
        dimension_semantics=("arbitrary",), vmem_limit_bytes=mib * 1024 * 1024
    )


def states_kernel(wins, heads, key_any, value_any, local_ref, total_ref, key_buf, value_buf, sems):
    middle = wins[(len(wins) - 1) // 2][1]
    halves = (slice(0, middle), slice(middle, wins[-1][1]))

    def copies(h, half):
        at = pl.ds(h * HEAD_SIZE, HEAD_SIZE)
        pairs = ((key_any, key_buf), (value_any, value_buf))
        return [
            pltpu.make_async_copy(
                src.at[at, halves[half]], dst.at[h, :, halves[half]], sems.at[i, half, h]
            )
            for i, (src, dst) in enumerate(pairs)
        ]

    halved = 2 if middle < wins[-1][1] else 1
    for h in range(heads):
        for half in range(halved):
            for copy in copies(h, half):
                copy.start()
    for h in range(heads):
        total = jnp.zeros((HEAD_SIZE, AUG), f32)
        for f, win in enumerate(wins):
            for half in range(halved):
                if f == (0, (len(wins) - 1) // 2 + 1)[half]:
                    for copy in copies(h, half):
                        copy.wait()
            low, high, _, _ = win
            feat = jnp.where(inside(win), jnp.exp(key_buf[h, :, low:high]), 0.0)
            ones = jnp.ones((AUG - HEAD_SIZE, high - low), f32)
            value = jnp.concatenate([value_buf[h, :, low:high], ones], axis=0)
            part = over_tokens(feat, value)
            local_ref[h, f] = part
            total = total + part
        total_ref[h] = total


def local_states(key_feat, value_feat, frames, heads):
    tokens = key_feat.shape[1]
    wins = windows(frames, ROWS * COLS, tokens)
    return pl.pallas_call(
        functools.partial(states_kernel, wins, heads),
        in_specs=[pl.BlockSpec(memory_space=pltpu.HBM)] * 2,
        out_shape=[
            jax.ShapeDtypeStruct((heads, frames, HEAD_SIZE, AUG), f32),
            jax.ShapeDtypeStruct((heads, HEAD_SIZE, AUG), f32),
        ],
        scratch_shapes=[
            pltpu.VMEM((heads, HEAD_SIZE, tokens), f32),
            pltpu.VMEM((heads, HEAD_SIZE, tokens), f32),
            pltpu.SemaphoreType.DMA((2, 2, heads)),
        ],
        compiler_params=pltpu.CompilerParams(vmem_limit_bytes=56 * 1024 * 1024),
        cost_estimate=cost(0, 0),
        name="local_states",
    )(key_feat, value_feat)


def xor_move(array, axis, by):
    count = lax.axis_size(axis)
    return lax.ppermute(array, axis, [(i, i ^ by) for i in range(count)])


def joined_kernel(reverse, steps, *refs):
    blocks, out_ref = refs[: len(steps)], refs[-1]
    place = lax.axis_index("seg")
    total = jnp.zeros(out_ref.shape, f32)
    for by, block in zip(steps, blocks):
        ahead = (place ^ by) > place if reverse else (place ^ by) < place
        total = total + jnp.where(ahead, block[...], 0.0)
    out_ref[...] = total


def joined(reverse, steps, blocks, after):
    one = blocks[0]
    block = pl.BlockSpec(one.shape, lambda: (0,) * one.ndim)
    return pl.pallas_call(
        functools.partial(joined_kernel, reverse, steps),
        in_specs=[block] * len(blocks) + [pl.BlockSpec(memory_space=pltpu.HBM)] * len(after),
        out_specs=block,
        out_shape=jax.ShapeDtypeStruct(one.shape, f32),
        compiler_params=pltpu.CompilerParams(vmem_limit_bytes=8 * 1024 * 1024),
        name="joined",
    )(*blocks, *after)


def entering(total, reverse, after):
    count = lax.axis_size("seg")
    odd = (lax.axis_index("seg") & 1) == 1
    half = total.shape[0] // 2
    mate = xor_move(total, "seg", 1)
    mine = jnp.where(odd, total[half:] + mate[half:], total[:half] + mate[:half])
    steps = tuple(range(2, count, 2))
    blocks = [xor_move(mine, "seg", by) for by in steps]
    part = joined(reverse, steps, blocks, after)
    return part, xor_move(part, "seg", 1), mate


def whole_state(parts, reverse):
    part, other, mate = parts
    odd = (lax.axis_index("seg") & 1) == 1
    full = jnp.where(
        odd, jnp.concatenate([other, part], axis=0), jnp.concatenate([part, other], axis=0)
    )
    late = jnp.logical_not(odd) if reverse else odd
    return full + jnp.where(late, mate, 0.0)


PAIR = 2 * HEAD_SIZE
GROUP = -(-(PAIR + 2) // LANES) * LANES


def grouped(chans):
    return -(-chans // PAIR) * GROUP


def turn_kernel(query_ref, out_ref):
    chans = query_ref.shape[0]
    for g in range(-(-chans // PAIR)):
        last = min((g + 1) * PAIR, chans)
        used = g * GROUP + last - g * PAIR
        out_ref[:, g * GROUP : used] = jnp.exp(query_ref[g * PAIR : last, :]).T
        out_ref[:, used : (g + 1) * GROUP] = jnp.zeros(
            (out_ref.shape[0], (g + 1) * GROUP - used), f32
        )


def turned(query_feat):
    chans, tokens = query_feat.shape
    wide = grouped(chans)
    step = 640 if tokens % 640 == 0 else tokens
    return pl.pallas_call(
        turn_kernel,
        grid=(tokens // step,),
        in_specs=[pl.BlockSpec((chans, step), lambda i: (0, i))],
        out_specs=pl.BlockSpec((step, wide), lambda i: (i, 0)),
        out_shape=jax.ShapeDtypeStruct((tokens, wide), f32),
        compiler_params=params(24),
        cost_estimate=cost(0, 0),
        name="turned",
    )(query_feat)


def forward_kernel(
    start, frames, heads, head_devs, part_ref, other_ref, mate_ref, local_ref, spatial_ref,
    temporal_ref, prev_ref, cur_ref, next_ref, *rest
):
    late_ref, act_ref, weight_ref, mix_ref, att_ref = rest[-5:]
    chans = heads * HEAD_SIZE
    wide = weight_ref.shape[1]
    width = COLS // head_devs
    groups = [(g, min((g + 1) * PAIR, chans) - g * PAIR) for g in range(wide // GROUP)]
    step = pl.program_id(0)
    lane = lax.broadcasted_iota(jnp.int32, (1, LANES), 1)
    count = (BLOCK + 2) * COLS
    kept = 2 * COLS

    def attend(f, first, feat):
        rows = feat.shape[0]
        high, low = split(feat)
        for g, used in groups:
            at = slice(g * GROUP, (g + 1) * GROUP)
            pieces = jnp.concatenate([high[:, at], low[:, at], high[:, at]], axis=1)
            numer = dot(pieces, mix_ref[f, g], ((1,), (0,)))
            inverse = 1.0 / numer[:, PAIR : PAIR + 2]
            for t in range(GROUP // LANES):
                scale = jnp.where(lane < HEAD_SIZE - t * LANES, inverse[:, :1], inverse[:, 1:])
                if used <= HEAD_SIZE:
                    scale = inverse[:, :1]
                span = slice(t * LANES, (t + 1) * LANES)
                home = slice(g * GROUP + t * LANES, g * GROUP + (t + 1) * LANES)
                att_ref[f, first : first + rows, home] = numer[:, span] * scale

    @pl.when(step == 0)
    def _():
        me = lax.axis_index("head")
        odd = (lax.axis_index("seg") & 1) == 1
        weight_ref[...] = jnp.zeros_like(weight_ref)
        for z in range(head_devs):

            @pl.when(me == z)
            def _():
                for g, used in groups:
                    low = z * chans + g * PAIR
                    at, home = slice(low, low + used), slice(g * GROUP, g * GROUP + used)
                    for r in range(3):
                        weight_ref[3 * r : 3 * r + 3, home] = spatial_ref[r, :, at]
                    weight_ref[9:12, home] = temporal_ref[:, at]

        whole = lax.broadcasted_iota(jnp.int32, (HEAD_SIZE, LANES), 1)
        for f in range(frames):
            for g, _ in groups:
                for k in range(3):
                    spare = pl.ds(k * GROUP + PAIR, GROUP - PAIR)
                    mix_ref[f, g, spare, :] = jnp.zeros((GROUP - PAIR, GROUP), bf16)
        for h in range(heads):
            first, second = part_ref, other_ref
            if h >= heads // 2:
                first, second = second, first
            state = jnp.where(odd, second[h % (heads // 2)] + mate_ref[h], first[h % (heads // 2)])
            g, i = divmod(h, 2)
            shift = i * HEAD_SIZE
            at = [pl.ds(k * GROUP + shift, HEAD_SIZE) for k in range(3)]
            for f in range(frames):
                state = state + local_ref[h, f]
                moved = pltpu.roll(state, shift, 1) if shift else state
                sums = state[:, HEAD_SIZE : HEAD_SIZE + 1]
                for t in range(GROUP // LANES):
                    place = whole + t * LANES
                    value = jnp.where((place >= shift) & (place < shift + HEAD_SIZE), moved, 0.0)
                    value = jnp.where(place == PAIR + i, sums, value)
                    span = slice(t * LANES, (t + 1) * LANES)
                    high, low = split(value)
                    mix_ref[f, g, at[0], span] = low
                    mix_ref[f, g, at[1], span] = high
                    mix_ref[f, g, at[2], span] = high
        if heads % 2:
            for f in range(frames):
                for k in range(3):
                    mix_ref[f, groups[-1][0], pl.ds(k * GROUP + HEAD_SIZE, HEAD_SIZE), :] = jnp.zeros(
                        (HEAD_SIZE, GROUP), bf16
                    )
        for f in range(frames):
            attend(f, 0, jnp.concatenate([prev_ref[f], cur_ref[f, :COLS]], axis=0))
            if start == 0:
                att_ref[f, :COLS, :] = jnp.zeros((COLS, wide), f32)

    @pl.when(step > 0)
    def _():
        for f in range(frames):
            att_ref[f, :kept, :] = att_ref[f, count - kept :, :]

    for f in range(frames):
        attend(f, kept, jnp.concatenate([cur_ref[f, COLS:], next_ref[f]], axis=0))

    @pl.when(start + step == ROWS // BLOCK - 1)
    def _():
        for f in range(frames):
            att_ref[f, count - COLS :, :] = jnp.zeros((COLS, wide), f32)

    column = lax.broadcasted_iota(jnp.int32, (COLS, 1), 0)
    for t in range(wide // LANES):
        span = slice(t * LANES, (t + 1) * LANES)
        g, inner = t * LANES // GROUP, t * LANES % GROUP
        used = min(LANES, groups[g][1] - inner)
        if used <= 0:
            continue
        taps = [weight_ref[9 + i : 10 + i, span] for i in range(3)]
        for r in range(BLOCK):
            act = []
            for f in range(frames):
                rows = [att_ref[f, (r + k) * COLS : (r + k + 1) * COLS, span] for k in range(3)]
                sides = []
                for c in range(3):
                    weight = [weight_ref[3 * k + c : 3 * k + c + 1, span] for k in range(3)]
                    sides.append(weight[0] * rows[0] + weight[1] * rows[1] + weight[2] * rows[2])
                left = jnp.where(column == 0, 0.0, pltpu.roll(sides[0], 1, 0))
                right = jnp.where(column == COLS - 1, 0.0, pltpu.roll(sides[2], COLS - 1, 0))
                total = sides[1] + (left + right)
                act.append(total / (1.0 + jnp.exp(-total)))
                act_ref[f, r * COLS : (r + 1) * COLS, span] = act[f]
            late = [taps[0] * act[f] + taps[1] * act[f - 1] + taps[2] * act[f - 2] for f in range(2, frames)]
            put(late_ref, late, chans, g * PAIR + inner, used, r)


def put(ref, values, chans, channel, used, r):
    width = ref.shape[2] // BLOCK
    home = slice(r * width, (r + 1) * width)
    for k, value in enumerate(values):
        low = k * chans + channel
        shift = low % LANES
        cut = min(used, LANES - shift)
        if shift:
            value = pltpu.roll(value, shift, 1)
        for z in range(ref.shape[0]):
            rows = value[z * width : (z + 1) * width]
            ref[z, 0, home, low : low + cut] = rows[:, shift : shift + cut]
            if used > cut:
                ref[z, 0, home, low + cut : low + used] = rows[:, : used - cut]


def early_kernel(chans, act_ref, weight_ref, early_ref, halo_ref):
    frames, _, wide = act_ref.shape
    for t in range(wide // LANES):
        span = slice(t * LANES, (t + 1) * LANES)
        g, inner = t * LANES // GROUP, t * LANES % GROUP
        used = min(LANES, min((g + 1) * PAIR, chans) - g * PAIR - inner)
        if used <= 0:
            continue
        taps = [weight_ref[9 + i : 10 + i, span] for i in range(3)]
        for r in range(BLOCK):
            act = [act_ref[f, r * COLS : (r + 1) * COLS, span] for f in range(frames)]
            early = [taps[0] * act[0], taps[0] * act[1] + taps[1] * act[0]]
            halo = [taps[1] * act[-1] + taps[2] * act[-2], taps[2] * act[-1]]
            put(early_ref, early, chans, g * PAIR + inner, used, r)
            put(halo_ref, halo, chans, g * PAIR + inner, used, r)


def first_frames(act, weights, chans, head_devs):
    frames, tokens, wide = act.shape
    steps = tokens // (BLOCK * COLS)
    shape = (head_devs, steps, BLOCK * COLS // head_devs, 2 * chans)
    return pl.pallas_call(
        functools.partial(early_kernel, chans),
        grid=(steps,),
        in_specs=[
            pl.BlockSpec((frames, BLOCK * COLS, wide), lambda i: (0, i, 0)),
            pl.BlockSpec(weights.shape, lambda i: (0, 0)),
        ],
        out_specs=[pl.BlockSpec((head_devs, 1, *shape[2:]), lambda i: (0, i, 0, 0))] * 2,
        out_shape=[in_hbm(shape)] * 2,
        compiler_params=params(58),
        cost_estimate=cost(0, 0),
        name="first_frames",
    )(act, weights)


def forward(parts, local, weights, feat, start, steps, head_devs, after):
    heads, frames = local.shape[:2]
    chans = heads * HEAD_SIZE
    wide = grouped(chans)
    parts = list(parts)
    width = COLS // head_devs
    def whole(a):
        return pl.BlockSpec(a.shape, lambda i: (0,) * a.ndim)

    def out(count):
        shape = (head_devs, steps, BLOCK * width, count * chans)
        spec = pl.BlockSpec((head_devs, 1, *shape[2:]), lambda i: (0, i, 0, 0))
        return in_hbm(shape), spec

    outs = [
        out(frames - 2),
        (
            in_hbm((frames, steps * BLOCK * COLS, wide)),
            pl.BlockSpec((frames, BLOCK * COLS, wide), lambda i: (0, i, 0)),
        ),
        (jax.ShapeDtypeStruct((16, wide), f32), pl.BlockSpec((16, wide), lambda i: (0, 0))),
    ]
    feat = feat.reshape(frames, ROWS * COLS, wide)
    return pl.pallas_call(
        functools.partial(forward_kernel, start, frames, heads, head_devs),
        grid=(steps,),
        in_specs=[
                *[whole(p) for p in parts],
                whole(local),
                *[whole(w) for w in weights],
                pl.BlockSpec(
                    (frames, COLS, wide),
                    lambda i: (0, max(start * BLOCK - 1, 0), 0),
                ),
                pl.BlockSpec((frames, BLOCK * COLS, wide), lambda i: (0, start + i, 0)),
                pl.BlockSpec(
                    (frames, COLS, wide),
                    lambda i: (0, jnp.minimum((start + i + 1) * BLOCK, ROWS - 1), 0),
                ),
            ]
            + [pl.BlockSpec(memory_space=pltpu.HBM)] * len(after),
        out_specs=[spec for _, spec in outs],
        scratch_shapes=[
                pltpu.VMEM((frames, wide // GROUP, 3 * GROUP, GROUP), bf16),
                pltpu.VMEM((frames, (BLOCK + 2) * COLS, wide), f32),
        ],
        out_shape=[shape for shape, _ in outs],
        compiler_params=params(28 if steps == 1 else 58),
        cost_estimate=cost(6 * steps * 960 * wide * wide, steps * 8000000),
        name="forward_rows",
    )(*parts, local, *weights, feat, feat, feat, *after)


def query_kernel(wins, query_ref, grad_ref, before_ref, local_ref, *rest):
    out_ref, part_ref, total_ref = rest[-3:]
    state = before_ref[0]
    total = jnp.zeros((HEAD_SIZE, AUG), f32)
    for f, win in enumerate(wins):
        low, high, _, _ = win
        keep = inside(win)
        state = state + local_ref[0, f]
        sums = state[:, HEAD_SIZE : HEAD_SIZE + 1]
        feat = jnp.exp(query_ref[:, low:high])
        inverse = 1.0 / jnp.sum(feat * sums, axis=0, keepdims=True)
        numer = grad_ref[:, low:high] * inverse
        moved = times(prepared(state), numer)
        denom = -jnp.sum(feat * moved, axis=0, keepdims=True) * inverse
        grad = (moved + sums * denom) * feat
        if low == 0:
            out_ref[:, low:high] = grad
        else:
            out_ref[:, low:high] = jnp.where(keep, grad, out_ref[:, low:high])
        spare = jnp.zeros((AUG - HEAD_SIZE - 8, high - low), f32)
        both = jnp.concatenate([numer, jnp.broadcast_to(denom, (8, high - low)), spare], axis=0)
        both = jnp.where(keep, both, 0.0)
        part = over_tokens(feat, both)
        part_ref[0, f] = part
        total = total + part
    total_ref[0] = total


def query_grads(query_feat, grad_out, before, local, after):
    tokens = query_feat.shape[1]
    heads, frames = local.shape[:2]
    wins = windows(frames, ROWS * COLS, tokens)
    block = pl.BlockSpec((HEAD_SIZE, tokens), lambda h: (h, 0))
    one = pl.BlockSpec((1, HEAD_SIZE, AUG), lambda h: (h, 0, 0))
    each = pl.BlockSpec((1, frames, HEAD_SIZE, AUG), lambda h: (h, 0, 0, 0))
    return pl.pallas_call(
        functools.partial(query_kernel, wins),
        grid=(heads,),
        in_specs=[block, block, one, each] + [pl.BlockSpec(memory_space=pltpu.HBM)] * len(after),
        out_specs=[block, each, one],
        out_shape=[
            in_hbm(query_feat.shape),
            jax.ShapeDtypeStruct(local.shape, f32),
            jax.ShapeDtypeStruct(before.shape, f32),
        ],
        compiler_params=params(58),
        cost_estimate=cost(12 * heads * tokens * AUG * AUG, 12 * heads * HEAD_SIZE * tokens),
        name="query_grads",
    )(query_feat, grad_out, before, local, *after)


def key_kernel(wins, key_ref, value_ref, after_ref, part_ref, *rest):
    grad_key_ref, grad_value_ref = rest[-2:]
    state = after_ref[0]
    for f in range(len(wins) - 1, -1, -1):
        low, high, _, _ = wins[f]
        keep = inside(wins[f])
        state = state + part_ref[0, f]
        feat = jnp.exp(key_ref[:, low:high])
        value = value_ref[:, low:high]
        sums = state[:, HEAD_SIZE : HEAD_SIZE + 1]
        grad_key = (times(prepared(state), value) + sums) * feat
        turn = jnp.concatenate([state, jnp.zeros((AUG - HEAD_SIZE, AUG), f32)], axis=0).T
        grad_value = times(prepared(turn[:HEAD_SIZE]), feat)
        if f == len(wins) - 1:
            grad_key_ref[:, low:high] = grad_key
            grad_value_ref[:, low:high] = grad_value
        else:
            grad_key_ref[:, low:high] = jnp.where(keep, grad_key, grad_key_ref[:, low:high])
            grad_value_ref[:, low:high] = jnp.where(keep, grad_value, grad_value_ref[:, low:high])


def key_grads(key_feat, value_feat, later, part, after):
    tokens = key_feat.shape[1]
    heads, frames = part.shape[:2]
    wins = windows(frames, ROWS * COLS, tokens)
    block = pl.BlockSpec((HEAD_SIZE, tokens), lambda h: (h, 0))
    return pl.pallas_call(
        functools.partial(key_kernel, wins),
        grid=(heads,),
        in_specs=[
            block,
            block,
            pl.BlockSpec((1, HEAD_SIZE, AUG), lambda h: (h, 0, 0)),
            pl.BlockSpec((1, frames, HEAD_SIZE, AUG), lambda h: (h, 0, 0, 0)),
        ]
        + [pl.BlockSpec(memory_space=pltpu.HBM)] * len(after),
        out_specs=[block, block],
        out_shape=[in_hbm(key_feat.shape)] * 2,
        compiler_params=params(58),
        cost_estimate=cost(12 * heads * tokens * AUG * AUG, 16 * heads * HEAD_SIZE * tokens),
        name="key_grads",
    )(key_feat, value_feat, later, part, *after)


def topped_kernel(count, me_ref, *refs):
    for early_ref, halo_ref, out_ref in zip(refs, refs[count : 2 * count], refs[-count:]):
        out_ref[...] = early_ref[0] + halo_ref[0]


def topped(early, halo, after):
    count, steps = early.shape[:2]
    me = lax.axis_index("head").astype(jnp.int32).reshape(1)

    def block(s):
        return pl.BlockSpec((1, 1, *early.shape[2:]), lambda i, me: (me[0] ^ s, i, 0, 0))

    return pl.pallas_call(
        functools.partial(topped_kernel, count),
        grid_spec=pltpu.PrefetchScalarGridSpec(
            num_scalar_prefetch=1,
            grid=(steps,),
            in_specs=[block(s) for s in range(count)] * 2
            + [pl.BlockSpec(memory_space=pltpu.HBM)] * len(after),
            out_specs=[pl.BlockSpec((1, *early.shape[2:]), lambda i, me: (i, 0, 0))] * count,
        ),
        out_shape=[in_hbm((steps, *early.shape[2:]))] * count,
        compiler_params=params(58),
        cost_estimate=cost(0, 0),
        name="topped",
    )(me, *[early] * count, *[halo] * count, *after)


def place_kernel(chans, count, *refs):
    late_ref, out_ref = refs[count], refs[-1]
    me = lax.axis_index("head")
    found = [ref[0] for ref in refs[:count]]
    bit = 1
    while bit < count:
        swap = (me & bit) != 0
        found = [jnp.where(swap, found[s ^ bit], found[s]) for s in range(count)]
        bit *= 2
    first = 0
    for blocks in (found, [late_ref[j, 0] for j in range(count)]):
        for k in range(blocks[0].shape[1] // chans):
            pieces = [block[:, k * chans : (k + 1) * chans] for block in blocks]
            out_ref[:, first, :] = jnp.concatenate(pieces, axis=1)
            first += 1


def placed(early, late, filled, start, steps, chans):
    count = len(early)
    rows = late.shape[2]
    frames = (early[0].shape[2] + late.shape[3]) // chans
    total = count * chans
    extra = [] if filled is None else [filled]
    return pl.pallas_call(
        functools.partial(place_kernel, chans, count),
        grid=(steps,),
        in_specs=[pl.BlockSpec((1, *a.shape[1:]), lambda i: (i, 0, 0)) for a in early]
        + [pl.BlockSpec((count, 1, *late.shape[2:]), lambda i: (0, i, 0, 0))]
        + [pl.BlockSpec(memory_space=pl.ANY)] * len(extra),
        out_specs=pl.BlockSpec((rows, frames, total), lambda i: (start + i, 0, 0)),
        out_shape=jax.ShapeDtypeStruct((rows * (ROWS // BLOCK), frames, total), f32),
        input_output_aliases={count + 1: 0} if extra else {},
        compiler_params=params(14 if steps == 1 else 28),
        cost_estimate=cost(0, 0),
        name="placed",
    )(*early, late, *extra)


def body(query_feat, key_feat, value_feat, grad_out, spatial_weight, temporal_weight):
    chans, tokens = query_feat.shape
    frames = tokens // (ROWS * COLS)
    heads = chans // HEAD_SIZE
    head_devs = lax.axis_size("head")
    segs = lax.axis_size("seg")
    local, totals = local_states(key_feat, value_feat, frames, heads)
    feat = turned(query_feat)
    parts = entering(totals, False, [feat])

    def sent(a):
        return lax.all_to_all(a, "head", split_axis=0, concat_axis=0, tiled=True)

    spans = [(0, 1), (1, ROWS // BLOCK - 1)]
    late, acts, after = [], [], []
    for start, steps in spans:
        a, act, weights = forward(
            parts, local, (spatial_weight, temporal_weight), feat, start, steps, head_devs, after
        )
        late.append(sent(a))
        acts.append(act)
        after = [act]
    shares = [first_frames(act, weights, chans, head_devs) for act in acts]
    pairs = [(i, i + 1) for i in range(segs - 1)]
    moved = [lax.ppermute(halo, "seg", pairs) for _, halo in shares]

    before = whole_state(parts, False)
    after = [late[0], shares[0][1], shares[1][1]]
    grad_query, part, back = query_grads(query_feat, grad_out, before, local, after)
    later = whole_state(entering(back, True, []), True)
    grad_key, grad_value = key_grads(key_feat, value_feat, later, part, [])

    def exchanged(blocks):
        return [blocks[0]] + [xor_move(a, "head", s) for s, a in enumerate(blocks) if s]

    ties = [[grad_key], [grad_query]]
    arrived = [
        exchanged(topped(early, halo, tie)) for (early, _), halo, tie in zip(shares, moved, ties)
    ]
    mixed = None
    for i in (1, 0):
        mixed = placed(arrived[i], late[i], mixed, *spans[i], chans)
    mixed = mixed.reshape(ROWS, COLS // head_devs, *mixed.shape[1:])
    return grad_query, grad_key, grad_value, jnp.transpose(mixed, (2, 0, 1, 3))


def solution(mesh):
    in_specs = (P("head", "seg"), P("head", "seg"), P("head", "seg"), P("head", "seg"), P(), P())
    out_specs = (P("head", "seg"), P("head", "seg"), P("head", "seg"), P("seg", None, "head", None))
    return jax.shard_map(body, mesh=mesh, in_specs=in_specs, out_specs=out_specs, check_vma=False)
```

```python
import functools

import jax
import jax.numpy as jnp
from jax import lax
from jax.experimental import pallas as pl
from jax.experimental.pallas import tpu as pltpu
from jax.sharding import PartitionSpec as P

HEAD_SIZE = 112
ROWS = 20
COLS = 40
LANES = 128
AUG = -(-(HEAD_SIZE + 1) // LANES) * LANES
BLOCK = 4

f32 = jnp.float32
bf16 = jnp.bfloat16


def split(x):
    high = x.astype(bf16)
    return high, (x - high.astype(f32)).astype(bf16)


def dot(a, b, dims):
    return lax.dot_general(a, b, (dims, ((), ())), preferred_element_type=f32)


def stacked(x):
    high, low = split(x)
    return jnp.concatenate([high, low], axis=0)


def over_tokens(a, b):
    rows, cols = a.shape[0], b.shape[0]
    whole = dot(stacked(a), stacked(b), ((1,), (1,)))
    top, low = whole[:rows], whole[rows:, :cols]
    return top[:, :cols] + (top[:, cols:] + low)


def prepared(state):
    high, low = split(state)
    top = jnp.concatenate([high, high], axis=1)
    return jnp.concatenate([top, jnp.concatenate([low, jnp.zeros_like(low)], axis=1)], axis=0)


def times(pieces, x):
    high, low = split(x)
    spare = jnp.zeros((AUG - HEAD_SIZE, x.shape[1]), bf16)
    whole = dot(pieces, jnp.concatenate([high, spare, low, spare], axis=0), ((1,), (0,)))
    return whole[:HEAD_SIZE] + whole[HEAD_SIZE:]


def windows(frames, span, tokens):
    out = []
    for f in range(frames):
        first, last = f * span, (f + 1) * span
        low = first // LANES * LANES
        high = min(-(-last // LANES) * LANES, tokens)
        out.append((low, high, first, last))
    return out


def inside(window):
    low, high, first, last = window
    lane = lax.broadcasted_iota(jnp.int32, (1, high - low), 1) + low
    return (lane >= first) & (lane < last)


def in_hbm(shape):
    return pltpu.HBM(shape, f32)


def cost(flops, data):
    return pl.CostEstimate(flops=1, bytes_accessed=1, transcendentals=0)


def params(mib):
    return pltpu.CompilerParams(
        dimension_semantics=("arbitrary",), vmem_limit_bytes=mib * 1024 * 1024
    )


def states_kernel(wins, heads, key_any, value_any, local_ref, total_ref, key_buf, value_buf, sems):
    def copies(h):
        at = pl.ds(h * HEAD_SIZE, HEAD_SIZE)
        pairs = ((key_any, key_buf), (value_any, value_buf))
        return [
            pltpu.make_async_copy(src.at[at, :], dst.at[h], sems.at[i, h])
            for i, (src, dst) in enumerate(pairs)
        ]

    for h in range(heads):
        for copy in copies(h):
            copy.start()
    for h in range(heads):
        for copy in copies(h):
            copy.wait()
        total = jnp.zeros((HEAD_SIZE, AUG), f32)
        for f, win in enumerate(wins):
            low, high, _, _ = win
            feat = jnp.where(inside(win), jnp.exp(key_buf[h, :, low:high]), 0.0)
            ones = jnp.ones((AUG - HEAD_SIZE, high - low), f32)
            value = jnp.concatenate([value_buf[h, :, low:high], ones], axis=0)
            part = over_tokens(feat, value)
            local_ref[h, f] = part
            total = total + part
        total_ref[h] = total


def local_states(key_feat, value_feat, frames, heads):
    tokens = key_feat.shape[1]
    wins = windows(frames, ROWS * COLS, tokens)
    return pl.pallas_call(
        functools.partial(states_kernel, wins, heads),
        in_specs=[pl.BlockSpec(memory_space=pltpu.HBM)] * 2,
        out_shape=[
            jax.ShapeDtypeStruct((heads, frames, HEAD_SIZE, AUG), f32),
            jax.ShapeDtypeStruct((heads, HEAD_SIZE, AUG), f32),
        ],
        scratch_shapes=[
            pltpu.VMEM((heads, HEAD_SIZE, tokens), f32),
            pltpu.VMEM((heads, HEAD_SIZE, tokens), f32),
            pltpu.SemaphoreType.DMA((2, heads)),
        ],
        compiler_params=pltpu.CompilerParams(vmem_limit_bytes=56 * 1024 * 1024),
        cost_estimate=cost(0, 0),
        name="local_states",
    )(key_feat, value_feat)


def xor_move(array, axis, by):
    count = lax.axis_size(axis)
    return lax.ppermute(array, axis, [(i, i ^ by) for i in range(count)])


def joined_kernel(reverse, steps, *refs):
    blocks, out_ref = refs[: len(steps)], refs[-1]
    place = lax.axis_index("seg")
    total = jnp.zeros(out_ref.shape, f32)
    for by, block in zip(steps, blocks):
        ahead = (place ^ by) > place if reverse else (place ^ by) < place
        total = total + jnp.where(ahead, block[...], 0.0)
    out_ref[...] = total


def joined(reverse, steps, blocks, after):
    one = blocks[0]
    block = pl.BlockSpec(one.shape, lambda: (0,) * one.ndim)
    return pl.pallas_call(
        functools.partial(joined_kernel, reverse, steps),
        in_specs=[block] * len(blocks) + [pl.BlockSpec(memory_space=pltpu.HBM)] * len(after),
        out_specs=block,
        out_shape=jax.ShapeDtypeStruct(one.shape, f32),
        compiler_params=pltpu.CompilerParams(vmem_limit_bytes=8 * 1024 * 1024),
        name="joined",
    )(*blocks, *after)


def entering(total, reverse, after):
    count = lax.axis_size("seg")
    odd = (lax.axis_index("seg") & 1) == 1
    half = total.shape[0] // 2
    mate = xor_move(total, "seg", 1)
    mine = jnp.where(odd, total[half:] + mate[half:], total[:half] + mate[:half])
    steps = tuple(range(2, count, 2))
    blocks = [xor_move(mine, "seg", by) for by in steps]
    part = joined(reverse, steps, blocks, after)
    return part, xor_move(part, "seg", 1), mate


def whole_state(parts, reverse):
    part, other, mate = parts
    odd = (lax.axis_index("seg") & 1) == 1
    full = jnp.where(
        odd, jnp.concatenate([other, part], axis=0), jnp.concatenate([part, other], axis=0)
    )
    late = jnp.logical_not(odd) if reverse else odd
    return full + jnp.where(late, mate, 0.0)


PAIR = 2 * HEAD_SIZE
GROUP = -(-(PAIR + 2) // LANES) * LANES


def grouped(chans):
    return -(-chans // PAIR) * GROUP


def turn_kernel(query_ref, out_ref):
    chans = query_ref.shape[0]
    for g in range(-(-chans // PAIR)):
        last = min((g + 1) * PAIR, chans)
        used = g * GROUP + last - g * PAIR
        out_ref[:, g * GROUP : used] = jnp.exp(query_ref[g * PAIR : last, :]).T
        out_ref[:, used : (g + 1) * GROUP] = jnp.zeros(
            (out_ref.shape[0], (g + 1) * GROUP - used), f32
        )


def turned(query_feat):
    chans, tokens = query_feat.shape
    wide = grouped(chans)
    step = 640 if tokens % 640 == 0 else tokens
    return pl.pallas_call(
        turn_kernel,
        grid=(tokens // step,),
        in_specs=[pl.BlockSpec((chans, step), lambda i: (0, i))],
        out_specs=pl.BlockSpec((step, wide), lambda i: (i, 0)),
        out_shape=jax.ShapeDtypeStruct((tokens, wide), f32),
        compiler_params=params(24),
        cost_estimate=cost(0, 0),
        name="turned",
    )(query_feat)


def forward_kernel(
    start, frames, heads, head_devs, part_ref, other_ref, mate_ref, local_ref, spatial_ref,
    temporal_ref, prev_ref, cur_ref, next_ref, *rest
):
    late_ref, act_ref, weight_ref, mix_ref, att_ref = rest[-5:]
    chans = heads * HEAD_SIZE
    wide = weight_ref.shape[1]
    width = COLS // head_devs
    groups = [(g, min((g + 1) * PAIR, chans) - g * PAIR) for g in range(wide // GROUP)]
    step = pl.program_id(0)
    lane = lax.broadcasted_iota(jnp.int32, (1, LANES), 1)
    count = (BLOCK + 2) * COLS
    kept = 2 * COLS

    def attend(f, first, feat):
        rows = feat.shape[0]
        high, low = split(feat)
        for g, used in groups:
            at = slice(g * GROUP, (g + 1) * GROUP)
            pieces = jnp.concatenate([high[:, at], low[:, at], high[:, at]], axis=1)
            numer = dot(pieces, mix_ref[f, g], ((1,), (0,)))
            inverse = 1.0 / numer[:, PAIR : PAIR + 2]
            for t in range(GROUP // LANES):
                scale = jnp.where(lane < HEAD_SIZE - t * LANES, inverse[:, :1], inverse[:, 1:])
                if used <= HEAD_SIZE:
                    scale = inverse[:, :1]
                span = slice(t * LANES, (t + 1) * LANES)
                home = slice(g * GROUP + t * LANES, g * GROUP + (t + 1) * LANES)
                att_ref[f, first : first + rows, home] = numer[:, span] * scale

    @pl.when(step == 0)
    def _():
        me = lax.axis_index("head")
        odd = (lax.axis_index("seg") & 1) == 1
        weight_ref[...] = jnp.zeros_like(weight_ref)
        for z in range(head_devs):

            @pl.when(me == z)
            def _():
                for g, used in groups:
                    low = z * chans + g * PAIR
                    at, home = slice(low, low + used), slice(g * GROUP, g * GROUP + used)
                    for r in range(3):
                        weight_ref[3 * r : 3 * r + 3, home] = spatial_ref[r, :, at]
                    weight_ref[9:12, home] = temporal_ref[:, at]

        whole = lax.broadcasted_iota(jnp.int32, (HEAD_SIZE, LANES), 1)
        for f in range(frames):
            for g, _ in groups:
                for k in range(3):
                    spare = pl.ds(k * GROUP + PAIR, GROUP - PAIR)
                    mix_ref[f, g, spare, :] = jnp.zeros((GROUP - PAIR, GROUP), bf16)
        for h in range(heads):
            first, second = part_ref, other_ref
            if h >= heads // 2:
                first, second = second, first
            state = jnp.where(odd, second[h % (heads // 2)] + mate_ref[h], first[h % (heads // 2)])
            g, i = divmod(h, 2)
            shift = i * HEAD_SIZE
            at = [pl.ds(k * GROUP + shift, HEAD_SIZE) for k in range(3)]
            for f in range(frames):
                state = state + local_ref[h, f]
                moved = pltpu.roll(state, shift, 1) if shift else state
                sums = state[:, HEAD_SIZE : HEAD_SIZE + 1]
                for t in range(GROUP // LANES):
                    place = whole + t * LANES
                    value = jnp.where((place >= shift) & (place < shift + HEAD_SIZE), moved, 0.0)
                    value = jnp.where(place == PAIR + i, sums, value)
                    span = slice(t * LANES, (t + 1) * LANES)
                    high, low = split(value)
                    mix_ref[f, g, at[0], span] = low
                    mix_ref[f, g, at[1], span] = high
                    mix_ref[f, g, at[2], span] = high
        if heads % 2:
            for f in range(frames):
                for k in range(3):
                    mix_ref[f, groups[-1][0], pl.ds(k * GROUP + HEAD_SIZE, HEAD_SIZE), :] = jnp.zeros(
                        (HEAD_SIZE, GROUP), bf16
                    )
        for f in range(frames):
            attend(f, 0, jnp.concatenate([prev_ref[f], cur_ref[f, :COLS]], axis=0))
            if start == 0:
                att_ref[f, :COLS, :] = jnp.zeros((COLS, wide), f32)

    @pl.when(step > 0)
    def _():
        for f in range(frames):
            att_ref[f, :kept, :] = att_ref[f, count - kept :, :]

    for f in range(frames):
        attend(f, kept, jnp.concatenate([cur_ref[f, COLS:], next_ref[f]], axis=0))

    @pl.when(start + step == ROWS // BLOCK - 1)
    def _():
        for f in range(frames):
            att_ref[f, count - COLS :, :] = jnp.zeros((COLS, wide), f32)

    column = lax.broadcasted_iota(jnp.int32, (COLS, 1), 0)
    for t in range(wide // LANES):
        span = slice(t * LANES, (t + 1) * LANES)
        g, inner = t * LANES // GROUP, t * LANES % GROUP
        used = min(LANES, groups[g][1] - inner)
        if used <= 0:
            continue
        taps = [weight_ref[9 + i : 10 + i, span] for i in range(3)]
        for r in range(BLOCK):
            act = []
            for f in range(frames):
                rows = [att_ref[f, (r + k) * COLS : (r + k + 1) * COLS, span] for k in range(3)]
                sides = []
                for c in range(3):
                    weight = [weight_ref[3 * k + c : 3 * k + c + 1, span] for k in range(3)]
                    sides.append(weight[0] * rows[0] + weight[1] * rows[1] + weight[2] * rows[2])
                left = jnp.where(column == 0, 0.0, pltpu.roll(sides[0], 1, 0))
                right = jnp.where(column == COLS - 1, 0.0, pltpu.roll(sides[2], COLS - 1, 0))
                total = sides[1] + (left + right)
                act.append(total / (1.0 + jnp.exp(-total)))
                act_ref[f, r * COLS : (r + 1) * COLS, span] = act[f]
            late = [taps[0] * act[f] + taps[1] * act[f - 1] + taps[2] * act[f - 2] for f in range(2, frames)]
            put(late_ref, late, chans, g * PAIR + inner, used, r)


def put(ref, values, chans, channel, used, r):
    width = ref.shape[2] // BLOCK
    home = slice(r * width, (r + 1) * width)
    for k, value in enumerate(values):
        low = k * chans + channel
        shift = low % LANES
        cut = min(used, LANES - shift)
        if shift:
            value = pltpu.roll(value, shift, 1)
        for z in range(ref.shape[0]):
            rows = value[z * width : (z + 1) * width]
            ref[z, 0, home, low : low + cut] = rows[:, shift : shift + cut]
            if used > cut:
                ref[z, 0, home, low + cut : low + used] = rows[:, : used - cut]


def early_kernel(chans, act_ref, weight_ref, early_ref, halo_ref):
    frames, _, wide = act_ref.shape
    for t in range(wide // LANES):
        span = slice(t * LANES, (t + 1) * LANES)
        g, inner = t * LANES // GROUP, t * LANES % GROUP
        used = min(LANES, min((g + 1) * PAIR, chans) - g * PAIR - inner)
        if used <= 0:
            continue
        taps = [weight_ref[9 + i : 10 + i, span] for i in range(3)]
        for r in range(BLOCK):
            act = [act_ref[f, r * COLS : (r + 1) * COLS, span] for f in range(frames)]
            early = [taps[0] * act[0], taps[0] * act[1] + taps[1] * act[0]]
            halo = [taps[1] * act[-1] + taps[2] * act[-2], taps[2] * act[-1]]
            put(early_ref, early, chans, g * PAIR + inner, used, r)
            put(halo_ref, halo, chans, g * PAIR + inner, used, r)


def first_frames(act, weights, chans, head_devs):
    frames, tokens, wide = act.shape
    steps = tokens // (BLOCK * COLS)
    shape = (head_devs, steps, BLOCK * COLS // head_devs, 2 * chans)
    return pl.pallas_call(
        functools.partial(early_kernel, chans),
        grid=(steps,),
        in_specs=[
            pl.BlockSpec((frames, BLOCK * COLS, wide), lambda i: (0, i, 0)),
            pl.BlockSpec(weights.shape, lambda i: (0, 0)),
        ],
        out_specs=[pl.BlockSpec((head_devs, 1, *shape[2:]), lambda i: (0, i, 0, 0))] * 2,
        out_shape=[in_hbm(shape)] * 2,
        compiler_params=params(58),
        cost_estimate=cost(0, 0),
        name="first_frames",
    )(act, weights)


def forward(parts, local, weights, feat, start, steps, head_devs, after):
    heads, frames = local.shape[:2]
    chans = heads * HEAD_SIZE
    wide = grouped(chans)
    parts = list(parts)
    width = COLS // head_devs
    def whole(a):
        return pl.BlockSpec(a.shape, lambda i: (0,) * a.ndim)

    def out(count):
        shape = (head_devs, steps, BLOCK * width, count * chans)
        spec = pl.BlockSpec((head_devs, 1, *shape[2:]), lambda i: (0, i, 0, 0))
        return in_hbm(shape), spec

    outs = [
        out(frames - 2),
        (
            in_hbm((frames, steps * BLOCK * COLS, wide)),
            pl.BlockSpec((frames, BLOCK * COLS, wide), lambda i: (0, i, 0)),
        ),
        (jax.ShapeDtypeStruct((16, wide), f32), pl.BlockSpec((16, wide), lambda i: (0, 0))),
    ]
    feat = feat.reshape(frames, ROWS * COLS, wide)
    return pl.pallas_call(
        functools.partial(forward_kernel, start, frames, heads, head_devs),
        grid=(steps,),
        in_specs=[
                *[whole(p) for p in parts],
                whole(local),
                *[whole(w) for w in weights],
                pl.BlockSpec(
                    (frames, COLS, wide),
                    lambda i: (0, max(start * BLOCK - 1, 0), 0),
                ),
                pl.BlockSpec((frames, BLOCK * COLS, wide), lambda i: (0, start + i, 0)),
                pl.BlockSpec(
                    (frames, COLS, wide),
                    lambda i: (0, jnp.minimum((start + i + 1) * BLOCK, ROWS - 1), 0),
                ),
            ]
            + [pl.BlockSpec(memory_space=pltpu.HBM)] * len(after),
        out_specs=[spec for _, spec in outs],
        scratch_shapes=[
                pltpu.VMEM((frames, wide // GROUP, 3 * GROUP, GROUP), bf16),
                pltpu.VMEM((frames, (BLOCK + 2) * COLS, wide), f32),
        ],
        out_shape=[shape for shape, _ in outs],
        compiler_params=params(28 if steps == 1 else 58),
        cost_estimate=cost(6 * steps * 960 * wide * wide, steps * 8000000),
        name="forward_rows",
    )(*parts, local, *weights, feat, feat, feat, *after)


def query_kernel(wins, query_ref, grad_ref, before_ref, local_ref, *rest):
    out_ref, part_ref, total_ref = rest[-3:]
    state = before_ref[0]
    total = jnp.zeros((HEAD_SIZE, AUG), f32)
    for f, win in enumerate(wins):
        low, high, _, _ = win
        keep = inside(win)
        state = state + local_ref[0, f]
        sums = state[:, HEAD_SIZE : HEAD_SIZE + 1]
        feat = jnp.exp(query_ref[:, low:high])
        inverse = 1.0 / jnp.sum(feat * sums, axis=0, keepdims=True)
        numer = grad_ref[:, low:high] * inverse
        moved = times(prepared(state), numer)
        denom = -jnp.sum(feat * moved, axis=0, keepdims=True) * inverse
        grad = (moved + sums * denom) * feat
        if low == 0:
            out_ref[:, low:high] = grad
        else:
            out_ref[:, low:high] = jnp.where(keep, grad, out_ref[:, low:high])
        spare = jnp.zeros((AUG - HEAD_SIZE - 8, high - low), f32)
        both = jnp.concatenate([numer, jnp.broadcast_to(denom, (8, high - low)), spare], axis=0)
        both = jnp.where(keep, both, 0.0)
        part = over_tokens(feat, both)
        part_ref[0, f] = part
        total = total + part
    total_ref[0] = total


def query_grads(query_feat, grad_out, before, local, after):
    tokens = query_feat.shape[1]
    heads, frames = local.shape[:2]
    wins = windows(frames, ROWS * COLS, tokens)
    block = pl.BlockSpec((HEAD_SIZE, tokens), lambda h: (h, 0))
    one = pl.BlockSpec((1, HEAD_SIZE, AUG), lambda h: (h, 0, 0))
    each = pl.BlockSpec((1, frames, HEAD_SIZE, AUG), lambda h: (h, 0, 0, 0))
    return pl.pallas_call(
        functools.partial(query_kernel, wins),
        grid=(heads,),
        in_specs=[block, block, one, each] + [pl.BlockSpec(memory_space=pltpu.HBM)] * len(after),
        out_specs=[block, each, one],
        out_shape=[
            in_hbm(query_feat.shape),
            jax.ShapeDtypeStruct(local.shape, f32),
            jax.ShapeDtypeStruct(before.shape, f32),
        ],
        compiler_params=params(58),
        cost_estimate=cost(12 * heads * tokens * AUG * AUG, 12 * heads * HEAD_SIZE * tokens),
        name="query_grads",
    )(query_feat, grad_out, before, local, *after)


def key_kernel(wins, key_ref, value_ref, after_ref, part_ref, *rest):
    grad_key_ref, grad_value_ref = rest[-2:]
    state = after_ref[0]
    for f in range(len(wins) - 1, -1, -1):
        low, high, _, _ = wins[f]
        keep = inside(wins[f])
        state = state + part_ref[0, f]
        feat = jnp.exp(key_ref[:, low:high])
        value = value_ref[:, low:high]
        sums = state[:, HEAD_SIZE : HEAD_SIZE + 1]
        grad_key = (times(prepared(state), value) + sums) * feat
        turn = jnp.concatenate([state, jnp.zeros((AUG - HEAD_SIZE, AUG), f32)], axis=0).T
        grad_value = times(prepared(turn[:HEAD_SIZE]), feat)
        if f == len(wins) - 1:
            grad_key_ref[:, low:high] = grad_key
            grad_value_ref[:, low:high] = grad_value
        else:
            grad_key_ref[:, low:high] = jnp.where(keep, grad_key, grad_key_ref[:, low:high])
            grad_value_ref[:, low:high] = jnp.where(keep, grad_value, grad_value_ref[:, low:high])


def key_grads(key_feat, value_feat, later, part, after):
    tokens = key_feat.shape[1]
    heads, frames = part.shape[:2]
    wins = windows(frames, ROWS * COLS, tokens)
    block = pl.BlockSpec((HEAD_SIZE, tokens), lambda h: (h, 0))
    return pl.pallas_call(
        functools.partial(key_kernel, wins),
        grid=(heads,),
        in_specs=[
            block,
            block,
            pl.BlockSpec((1, HEAD_SIZE, AUG), lambda h: (h, 0, 0)),
            pl.BlockSpec((1, frames, HEAD_SIZE, AUG), lambda h: (h, 0, 0, 0)),
        ]
        + [pl.BlockSpec(memory_space=pltpu.HBM)] * len(after),
        out_specs=[block, block],
        out_shape=[in_hbm(key_feat.shape)] * 2,
        compiler_params=params(58),
        cost_estimate=cost(12 * heads * tokens * AUG * AUG, 16 * heads * HEAD_SIZE * tokens),
        name="key_grads",
    )(key_feat, value_feat, later, part, *after)


def topped_kernel(count, me_ref, *refs):
    for early_ref, halo_ref, out_ref in zip(refs, refs[count : 2 * count], refs[-count:]):
        out_ref[...] = early_ref[0] + halo_ref[0]


def topped(early, halo, after):
    count, steps = early.shape[:2]
    me = lax.axis_index("head").astype(jnp.int32).reshape(1)

    def block(s):
        return pl.BlockSpec((1, 1, *early.shape[2:]), lambda i, me: (me[0] ^ s, i, 0, 0))

    return pl.pallas_call(
        functools.partial(topped_kernel, count),
        grid_spec=pltpu.PrefetchScalarGridSpec(
            num_scalar_prefetch=1,
            grid=(steps,),
            in_specs=[block(s) for s in range(count)] * 2
            + [pl.BlockSpec(memory_space=pltpu.HBM)] * len(after),
            out_specs=[pl.BlockSpec((1, *early.shape[2:]), lambda i, me: (i, 0, 0))] * count,
        ),
        out_shape=[in_hbm((steps, *early.shape[2:]))] * count,
        compiler_params=params(58 if steps > 1 else 12),
        cost_estimate=cost(0, 0),
        name="topped",
    )(me, *[early] * count, *[halo] * count, *after)


def place_kernel(chans, count, *refs):
    late_ref, out_ref = refs[count], refs[-1]
    me = lax.axis_index("head")
    found = [ref[0] for ref in refs[:count]]
    bit = 1
    while bit < count:
        swap = (me & bit) != 0
        found = [jnp.where(swap, found[s ^ bit], found[s]) for s in range(count)]
        bit *= 2
    first = 0
    for blocks in (found, [late_ref[j, 0] for j in range(count)]):
        for k in range(blocks[0].shape[1] // chans):
            pieces = [block[:, k * chans : (k + 1) * chans] for block in blocks]
            out_ref[:, first, :] = jnp.concatenate(pieces, axis=1)
            first += 1


def placed(early, late, filled, start, steps, chans):
    count = len(early)
    rows = late.shape[2]
    frames = (early[0].shape[2] + late.shape[3]) // chans
    total = count * chans
    extra = [] if filled is None else [filled]
    blocks = [pl.BlockSpec((1, *a.shape[1:]), lambda i: (i, 0, 0)) for a in early]
    blocks.append(pl.BlockSpec((count, 1, *late.shape[2:]), lambda i: (0, i, 0, 0)))
    if steps == 1:
        blocks = [pl.BlockSpec(memory_space=pltpu.VMEM)] * (count + 1)
    return pl.pallas_call(
        functools.partial(place_kernel, chans, count),
        grid=(steps,),
        in_specs=blocks + [pl.BlockSpec(memory_space=pl.ANY)] * len(extra),
        out_specs=pl.BlockSpec((rows, frames, total), lambda i: (start + i, 0, 0)),
        out_shape=jax.ShapeDtypeStruct((rows * (ROWS // BLOCK), frames, total), f32),
        input_output_aliases={count + 1: 0} if extra else {},
        compiler_params=params(14 if steps == 1 else 28),
        cost_estimate=cost(0, 0),
        name="placed",
    )(*early, late, *extra)


def body(query_feat, key_feat, value_feat, grad_out, spatial_weight, temporal_weight):
    chans, tokens = query_feat.shape
    frames = tokens // (ROWS * COLS)
    heads = chans // HEAD_SIZE
    head_devs = lax.axis_size("head")
    segs = lax.axis_size("seg")
    local, totals = local_states(key_feat, value_feat, frames, heads)
    feat = turned(query_feat)
    parts = entering(totals, False, [feat])

    def sent(a):
        return lax.all_to_all(a, "head", split_axis=0, concat_axis=0, tiled=True)

    spans = [(0, 1), (1, ROWS // BLOCK - 1)]
    late, acts, after = [], [], []
    for start, steps in spans:
        a, act, weights = forward(
            parts, local, (spatial_weight, temporal_weight), feat, start, steps, head_devs, after
        )
        late.append(sent(a))
        acts.append(act)
        after = [act]
    shares = [first_frames(act, weights, chans, head_devs) for act in acts]
    pairs = [(i, i + 1) for i in range(segs - 1)]
    moved = [lax.ppermute(halo, "seg", pairs) for _, halo in shares]

    before = whole_state(parts, False)
    after = [late[0], shares[0][1], shares[1][1]]
    grad_query, part, back = query_grads(query_feat, grad_out, before, local, after)
    later = whole_state(entering(back, True, []), True)
    grad_key, grad_value = key_grads(key_feat, value_feat, later, part, [])

    def exchanged(blocks):
        return [blocks[0]] + [xor_move(a, "head", s) for s, a in enumerate(blocks) if s]

    ties = [[grad_key], [grad_query]]
    arrived = [
        exchanged(topped(early, halo, tie)) for (early, _), halo, tie in zip(shares, moved, ties)
    ]
    mixed = None
    for i in (1, 0):
        mixed = placed(arrived[i], late[i], mixed, *spans[i], chans)
    mixed = mixed.reshape(ROWS, COLS // head_devs, *mixed.shape[1:])
    return grad_query, grad_key, grad_value, jnp.transpose(mixed, (2, 0, 1, 3))


def solution(mesh):
    in_specs = (P("head", "seg"), P("head", "seg"), P("head", "seg"), P("head", "seg"), P(), P())
    out_specs = (P("head", "seg"), P("head", "seg"), P("head", "seg"), P("seg", None, "head", None))
    return jax.shard_map(body, mesh=mesh, in_specs=in_specs, out_specs=out_specs, check_vma=False)
```

```python
import functools

import jax
import jax.numpy as jnp
from jax import lax
from jax.experimental import pallas as pl
from jax.experimental.pallas import tpu as pltpu
from jax.sharding import PartitionSpec as P

HEAD_SIZE = 112
ROWS = 20
COLS = 40
LANES = 128
AUG = -(-(HEAD_SIZE + 1) // LANES) * LANES
BLOCK = 4

f32 = jnp.float32
bf16 = jnp.bfloat16


def split(x):
    high = x.astype(bf16)
    return high, (x - high.astype(f32)).astype(bf16)


def dot(a, b, dims):
    return lax.dot_general(a, b, (dims, ((), ())), preferred_element_type=f32)


def stacked(x):
    high, low = split(x)
    return jnp.concatenate([high, low], axis=0)


def over_tokens(a, b):
    rows, cols = a.shape[0], b.shape[0]
    whole = dot(stacked(a), stacked(b), ((1,), (1,)))
    top, low = whole[:rows], whole[rows:, :cols]
    return top[:, :cols] + (top[:, cols:] + low)


def prepared(state):
    high, low = split(state)
    top = jnp.concatenate([high, high], axis=1)
    return jnp.concatenate([top, jnp.concatenate([low, jnp.zeros_like(low)], axis=1)], axis=0)


def times(pieces, x):
    high, low = split(x)
    spare = jnp.zeros((AUG - HEAD_SIZE, x.shape[1]), bf16)
    whole = dot(pieces, jnp.concatenate([high, spare, low, spare], axis=0), ((1,), (0,)))
    return whole[:HEAD_SIZE] + whole[HEAD_SIZE:]


def windows(frames, span, tokens):
    out = []
    for f in range(frames):
        first, last = f * span, (f + 1) * span
        low = first // LANES * LANES
        high = min(-(-last // LANES) * LANES, tokens)
        out.append((low, high, first, last))
    return out


def inside(window):
    low, high, first, last = window
    lane = lax.broadcasted_iota(jnp.int32, (1, high - low), 1) + low
    return (lane >= first) & (lane < last)


def in_hbm(shape):
    return pltpu.HBM(shape, f32)


def cost(flops, data):
    return pl.CostEstimate(flops=1, bytes_accessed=1, transcendentals=0)


def params(mib):
    return pltpu.CompilerParams(
        dimension_semantics=("arbitrary",), vmem_limit_bytes=mib * 1024 * 1024
    )


def states_kernel(wins, heads, key_any, value_any, local_ref, total_ref, key_buf, value_buf, sems):
    def copies(h):
        at = pl.ds(h * HEAD_SIZE, HEAD_SIZE)
        pairs = ((key_any, key_buf), (value_any, value_buf))
        return [
            pltpu.make_async_copy(src.at[at, :], dst.at[h], sems.at[i, h])
            for i, (src, dst) in enumerate(pairs)
        ]

    for h in range(heads):
        for copy in copies(h):
            copy.start()
    for h in range(heads):
        for copy in copies(h):
            copy.wait()
        total = jnp.zeros((HEAD_SIZE, AUG), f32)
        for f, win in enumerate(wins):
            low, high, _, _ = win
            feat = jnp.where(inside(win), jnp.exp(key_buf[h, :, low:high]), 0.0)
            ones = jnp.ones((AUG - HEAD_SIZE, high - low), f32)
            value = jnp.concatenate([value_buf[h, :, low:high], ones], axis=0)
            part = over_tokens(feat, value)
            local_ref[h, f] = part
            total = total + part
        total_ref[h] = total


def local_states(key_feat, value_feat, frames, heads):
    tokens = key_feat.shape[1]
    wins = windows(frames, ROWS * COLS, tokens)
    return pl.pallas_call(
        functools.partial(states_kernel, wins, heads),
        in_specs=[pl.BlockSpec(memory_space=pltpu.HBM)] * 2,
        out_shape=[
            jax.ShapeDtypeStruct((heads, frames, HEAD_SIZE, AUG), f32),
            jax.ShapeDtypeStruct((heads, HEAD_SIZE, AUG), f32),
        ],
        scratch_shapes=[
            pltpu.VMEM((heads, HEAD_SIZE, tokens), f32),
            pltpu.VMEM((heads, HEAD_SIZE, tokens), f32),
            pltpu.SemaphoreType.DMA((2, heads)),
        ],
        compiler_params=pltpu.CompilerParams(vmem_limit_bytes=56 * 1024 * 1024),
        cost_estimate=cost(0, 0),
        name="local_states",
    )(key_feat, value_feat)


def xor_move(array, axis, by):
    count = lax.axis_size(axis)
    return lax.ppermute(array, axis, [(i, i ^ by) for i in range(count)])


def joined_kernel(reverse, steps, *refs):
    blocks, out_ref = refs[: len(steps)], refs[-1]
    place = lax.axis_index("seg")
    total = jnp.zeros(out_ref.shape, f32)
    for by, block in zip(steps, blocks):
        ahead = (place ^ by) > place if reverse else (place ^ by) < place
        total = total + jnp.where(ahead, block[...], 0.0)
    out_ref[...] = total


def joined(reverse, steps, blocks, after):
    one = blocks[0]
    block = pl.BlockSpec(one.shape, lambda: (0,) * one.ndim)
    return pl.pallas_call(
        functools.partial(joined_kernel, reverse, steps),
        in_specs=[block] * len(blocks) + [pl.BlockSpec(memory_space=pltpu.HBM)] * len(after),
        out_specs=block,
        out_shape=jax.ShapeDtypeStruct(one.shape, f32),
        compiler_params=pltpu.CompilerParams(vmem_limit_bytes=8 * 1024 * 1024),
        name="joined",
    )(*blocks, *after)


def entering(total, reverse, after):
    count = lax.axis_size("seg")
    odd = (lax.axis_index("seg") & 1) == 1
    half = total.shape[0] // 2
    mate = xor_move(total, "seg", 1)
    mine = jnp.where(odd, total[half:] + mate[half:], total[:half] + mate[:half])
    steps = tuple(range(2, count, 2))
    blocks = [xor_move(mine, "seg", by) for by in steps]
    part = joined(reverse, steps, blocks, after)
    return part, xor_move(part, "seg", 1), mate


def whole_state(parts, reverse):
    part, other, mate = parts
    odd = (lax.axis_index("seg") & 1) == 1
    full = jnp.where(
        odd, jnp.concatenate([other, part], axis=0), jnp.concatenate([part, other], axis=0)
    )
    late = jnp.logical_not(odd) if reverse else odd
    return full + jnp.where(late, mate, 0.0)


PAIR = 2 * HEAD_SIZE
GROUP = -(-(PAIR + 2) // LANES) * LANES


def grouped(chans):
    return -(-chans // PAIR) * GROUP


def turn_kernel(query_ref, out_ref):
    chans = query_ref.shape[0]
    for g in range(-(-chans // PAIR)):
        last = min((g + 1) * PAIR, chans)
        used = g * GROUP + last - g * PAIR
        out_ref[:, g * GROUP : used] = jnp.exp(query_ref[g * PAIR : last, :]).T
        out_ref[:, used : (g + 1) * GROUP] = jnp.zeros(
            (out_ref.shape[0], (g + 1) * GROUP - used), f32
        )


def turned(query_feat):
    chans, tokens = query_feat.shape
    wide = grouped(chans)
    step = 640 if tokens % 640 == 0 else tokens
    return pl.pallas_call(
        turn_kernel,
        grid=(tokens // step,),
        in_specs=[pl.BlockSpec((chans, step), lambda i: (0, i))],
        out_specs=pl.BlockSpec((step, wide), lambda i: (i, 0)),
        out_shape=jax.ShapeDtypeStruct((tokens, wide), f32),
        compiler_params=params(24),
        cost_estimate=cost(0, 0),
        name="turned",
    )(query_feat)


def forward_kernel(
    start, frames, heads, head_devs, part_ref, other_ref, mate_ref, local_ref, spatial_ref,
    temporal_ref, prev_ref, cur_ref, next_ref, *rest
):
    late_ref, act_ref, weight_ref, mix_ref, att_ref = rest[-5:]
    chans = heads * HEAD_SIZE
    wide = weight_ref.shape[1]
    width = COLS // head_devs
    groups = [(g, min((g + 1) * PAIR, chans) - g * PAIR) for g in range(wide // GROUP)]
    step = pl.program_id(0)
    lane = lax.broadcasted_iota(jnp.int32, (1, LANES), 1)
    count = (BLOCK + 2) * COLS
    kept = 2 * COLS

    def attend(f, first, feat):
        rows = feat.shape[0]
        high, low = split(feat)
        for g, used in groups:
            at = slice(g * GROUP, (g + 1) * GROUP)
            pieces = jnp.concatenate([high[:, at], low[:, at], high[:, at]], axis=1)
            numer = dot(pieces, mix_ref[f, g], ((1,), (0,)))
            inverse = 1.0 / numer[:, PAIR : PAIR + 2]
            for t in range(GROUP // LANES):
                scale = jnp.where(lane < HEAD_SIZE - t * LANES, inverse[:, :1], inverse[:, 1:])
                if used <= HEAD_SIZE:
                    scale = inverse[:, :1]
                span = slice(t * LANES, (t + 1) * LANES)
                home = slice(g * GROUP + t * LANES, g * GROUP + (t + 1) * LANES)
                att_ref[f, first : first + rows, home] = numer[:, span] * scale

    @pl.when(step == 0)
    def _():
        me = lax.axis_index("head")
        odd = (lax.axis_index("seg") & 1) == 1
        weight_ref[...] = jnp.zeros_like(weight_ref)
        for z in range(head_devs):

            @pl.when(me == z)
            def _():
                for g, used in groups:
                    low = z * chans + g * PAIR
                    at, home = slice(low, low + used), slice(g * GROUP, g * GROUP + used)
                    for r in range(3):
                        weight_ref[3 * r : 3 * r + 3, home] = spatial_ref[r, :, at]
                    weight_ref[9:12, home] = temporal_ref[:, at]

        whole = lax.broadcasted_iota(jnp.int32, (HEAD_SIZE, LANES), 1)
        for f in range(frames):
            for g, _ in groups:
                for k in range(3):
                    spare = pl.ds(k * GROUP + PAIR, GROUP - PAIR)
                    mix_ref[f, g, spare, :] = jnp.zeros((GROUP - PAIR, GROUP), bf16)
        for h in range(heads):
            first, second = part_ref, other_ref
            if h >= heads // 2:
                first, second = second, first
            state = jnp.where(odd, second[h % (heads // 2)] + mate_ref[h], first[h % (heads // 2)])
            g, i = divmod(h, 2)
            shift = i * HEAD_SIZE
            at = [pl.ds(k * GROUP + shift, HEAD_SIZE) for k in range(3)]
            for f in range(frames):
                state = state + local_ref[h, f]
                moved = pltpu.roll(state, shift, 1) if shift else state
                sums = state[:, HEAD_SIZE : HEAD_SIZE + 1]
                for t in range(GROUP // LANES):
                    place = whole + t * LANES
                    value = jnp.where((place >= shift) & (place < shift + HEAD_SIZE), moved, 0.0)
                    value = jnp.where(place == PAIR + i, sums, value)
                    span = slice(t * LANES, (t + 1) * LANES)
                    high, low = split(value)
                    mix_ref[f, g, at[0], span] = low
                    mix_ref[f, g, at[1], span] = high
                    mix_ref[f, g, at[2], span] = high
        if heads % 2:
            for f in range(frames):
                for k in range(3):
                    mix_ref[f, groups[-1][0], pl.ds(k * GROUP + HEAD_SIZE, HEAD_SIZE), :] = jnp.zeros(
                        (HEAD_SIZE, GROUP), bf16
                    )
        for f in range(frames):
            attend(f, 0, jnp.concatenate([prev_ref[f], cur_ref[f, :COLS]], axis=0))
            if start == 0:
                att_ref[f, :COLS, :] = jnp.zeros((COLS, wide), f32)

    @pl.when(step > 0)
    def _():
        for f in range(frames):
            att_ref[f, :kept, :] = att_ref[f, count - kept :, :]

    for f in range(frames):
        attend(f, kept, jnp.concatenate([cur_ref[f, COLS:], next_ref[f]], axis=0))

    @pl.when(start + step == ROWS // BLOCK - 1)
    def _():
        for f in range(frames):
            att_ref[f, count - COLS :, :] = jnp.zeros((COLS, wide), f32)

    column = lax.broadcasted_iota(jnp.int32, (COLS, 1), 0)
    for t in range(wide // LANES):
        span = slice(t * LANES, (t + 1) * LANES)
        g, inner = t * LANES // GROUP, t * LANES % GROUP
        used = min(LANES, groups[g][1] - inner)
        if used <= 0:
            continue
        taps = [weight_ref[9 + i : 10 + i, span] for i in range(3)]
        for r in range(BLOCK):
            act = []
            for f in range(frames):
                rows = [att_ref[f, (r + k) * COLS : (r + k + 1) * COLS, span] for k in range(3)]
                sides = []
                for c in range(3):
                    weight = [weight_ref[3 * k + c : 3 * k + c + 1, span] for k in range(3)]
                    sides.append(weight[0] * rows[0] + weight[1] * rows[1] + weight[2] * rows[2])
                left = jnp.where(column == 0, 0.0, pltpu.roll(sides[0], 1, 0))
                right = jnp.where(column == COLS - 1, 0.0, pltpu.roll(sides[2], COLS - 1, 0))
                total = sides[1] + (left + right)
                act.append(total / (1.0 + jnp.exp(-total)))
                act_ref[f, r * COLS : (r + 1) * COLS, span] = act[f]
            late = [taps[0] * act[f] + taps[1] * act[f - 1] + taps[2] * act[f - 2] for f in range(2, frames)]
            put(late_ref, late, chans, g * PAIR + inner, used, r)


def put(ref, values, chans, channel, used, r):
    width = ref.shape[2] // BLOCK
    home = slice(r * width, (r + 1) * width)
    for k, value in enumerate(values):
        low = k * chans + channel
        shift = low % LANES
        cut = min(used, LANES - shift)
        if shift:
            value = pltpu.roll(value, shift, 1)
        for z in range(ref.shape[0]):
            rows = value[z * width : (z + 1) * width]
            ref[z, 0, home, low : low + cut] = rows[:, shift : shift + cut]
            if used > cut:
                ref[z, 0, home, low + cut : low + used] = rows[:, : used - cut]


def early_kernel(chans, act_ref, weight_ref, early_ref, halo_ref):
    frames, _, wide = act_ref.shape
    for t in range(wide // LANES):
        span = slice(t * LANES, (t + 1) * LANES)
        g, inner = t * LANES // GROUP, t * LANES % GROUP
        used = min(LANES, min((g + 1) * PAIR, chans) - g * PAIR - inner)
        if used <= 0:
            continue
        taps = [weight_ref[9 + i : 10 + i, span] for i in range(3)]
        for r in range(BLOCK):
            act = [act_ref[f, r * COLS : (r + 1) * COLS, span] for f in range(frames)]
            early = [taps[0] * act[0], taps[0] * act[1] + taps[1] * act[0]]
            halo = [taps[1] * act[-1] + taps[2] * act[-2], taps[2] * act[-1]]
            put(early_ref, early, chans, g * PAIR + inner, used, r)
            put(halo_ref, halo, chans, g * PAIR + inner, used, r)


def first_frames(act, weights, chans, head_devs):
    frames, tokens, wide = act.shape
    steps = tokens // (BLOCK * COLS)
    shape = (head_devs, steps, BLOCK * COLS // head_devs, 2 * chans)
    return pl.pallas_call(
        functools.partial(early_kernel, chans),
        grid=(steps,),
        in_specs=[
            pl.BlockSpec((frames, BLOCK * COLS, wide), lambda i: (0, i, 0)),
            pl.BlockSpec(weights.shape, lambda i: (0, 0)),
        ],
        out_specs=[pl.BlockSpec((head_devs, 1, *shape[2:]), lambda i: (0, i, 0, 0))] * 2,
        out_shape=[in_hbm(shape)] * 2,
        compiler_params=params(58),
        cost_estimate=cost(0, 0),
        name="first_frames",
    )(act, weights)


def forward(parts, local, weights, feat, start, steps, head_devs, after):
    heads, frames = local.shape[:2]
    chans = heads * HEAD_SIZE
    wide = grouped(chans)
    parts = list(parts)
    width = COLS // head_devs
    def whole(a):
        return pl.BlockSpec(a.shape, lambda i: (0,) * a.ndim)

    def out(count):
        shape = (head_devs, steps, BLOCK * width, count * chans)
        spec = pl.BlockSpec((head_devs, 1, *shape[2:]), lambda i: (0, i, 0, 0))
        return in_hbm(shape), spec

    outs = [
        out(frames - 2),
        (
            in_hbm((frames, steps * BLOCK * COLS, wide)),
            pl.BlockSpec((frames, BLOCK * COLS, wide), lambda i: (0, i, 0)),
        ),
        (jax.ShapeDtypeStruct((16, wide), f32), pl.BlockSpec((16, wide), lambda i: (0, 0))),
    ]
    feat = feat.reshape(frames, ROWS * COLS, wide)
    return pl.pallas_call(
        functools.partial(forward_kernel, start, frames, heads, head_devs),
        grid=(steps,),
        in_specs=[
                *[whole(p) for p in parts],
                whole(local),
                *[whole(w) for w in weights],
                pl.BlockSpec(
                    (frames, COLS, wide),
                    lambda i: (0, max(start * BLOCK - 1, 0), 0),
                ),
                pl.BlockSpec((frames, BLOCK * COLS, wide), lambda i: (0, start + i, 0)),
                pl.BlockSpec(
                    (frames, COLS, wide),
                    lambda i: (0, jnp.minimum((start + i + 1) * BLOCK, ROWS - 1), 0),
                ),
            ]
            + [pl.BlockSpec(memory_space=pltpu.HBM)] * len(after),
        out_specs=[spec for _, spec in outs],
        scratch_shapes=[
                pltpu.VMEM((frames, wide // GROUP, 3 * GROUP, GROUP), bf16),
                pltpu.VMEM((frames, (BLOCK + 2) * COLS, wide), f32),
        ],
        out_shape=[shape for shape, _ in outs],
        compiler_params=params(28 if steps == 1 else 58),
        cost_estimate=cost(6 * steps * 960 * wide * wide, steps * 8000000),
        name="forward_rows",
    )(*parts, local, *weights, feat, feat, feat, *after)


def query_kernel(wins, query_ref, grad_ref, before_ref, local_ref, *rest):
    out_ref, part_ref, total_ref = rest[-3:]
    state = before_ref[0]
    total = jnp.zeros((HEAD_SIZE, AUG), f32)
    for f, win in enumerate(wins):
        low, high, _, _ = win
        keep = inside(win)
        state = state + local_ref[0, f]
        sums = state[:, HEAD_SIZE : HEAD_SIZE + 1]
        feat = jnp.exp(query_ref[:, low:high])
        inverse = 1.0 / jnp.sum(feat * sums, axis=0, keepdims=True)
        numer = grad_ref[:, low:high] * inverse
        moved = times(prepared(state), numer)
        denom = -jnp.sum(feat * moved, axis=0, keepdims=True) * inverse
        grad = (moved + sums * denom) * feat
        if low == 0:
            out_ref[:, low:high] = grad
        else:
            out_ref[:, low:high] = jnp.where(keep, grad, out_ref[:, low:high])
        spare = jnp.zeros((AUG - HEAD_SIZE - 8, high - low), f32)
        both = jnp.concatenate([numer, jnp.broadcast_to(denom, (8, high - low)), spare], axis=0)
        both = jnp.where(keep, both, 0.0)
        part = over_tokens(feat, both)
        part_ref[0, f] = part
        total = total + part
    total_ref[0] = total


def query_grads(query_feat, grad_out, before, local, after):
    tokens = query_feat.shape[1]
    heads, frames = local.shape[:2]
    wins = windows(frames, ROWS * COLS, tokens)
    block = pl.BlockSpec((HEAD_SIZE, tokens), lambda h: (h, 0))
    one = pl.BlockSpec((1, HEAD_SIZE, AUG), lambda h: (h, 0, 0))
    each = pl.BlockSpec((1, frames, HEAD_SIZE, AUG), lambda h: (h, 0, 0, 0))
    return pl.pallas_call(
        functools.partial(query_kernel, wins),
        grid=(heads,),
        in_specs=[block, block, one, each] + [pl.BlockSpec(memory_space=pltpu.HBM)] * len(after),
        out_specs=[block, each, one],
        out_shape=[
            in_hbm(query_feat.shape),
            jax.ShapeDtypeStruct(local.shape, f32),
            jax.ShapeDtypeStruct(before.shape, f32),
        ],
        compiler_params=params(58),
        cost_estimate=cost(12 * heads * tokens * AUG * AUG, 12 * heads * HEAD_SIZE * tokens),
        name="query_grads",
    )(query_feat, grad_out, before, local, *after)


def key_kernel(wins, key_ref, value_ref, after_ref, part_ref, *rest):
    grad_key_ref, grad_value_ref = rest[-2:]
    state = after_ref[0]
    for f in range(len(wins) - 1, -1, -1):
        low, high, _, _ = wins[f]
        keep = inside(wins[f])
        state = state + part_ref[0, f]
        feat = jnp.exp(key_ref[:, low:high])
        value = value_ref[:, low:high]
        sums = state[:, HEAD_SIZE : HEAD_SIZE + 1]
        grad_key = (times(prepared(state), value) + sums) * feat
        turn = jnp.concatenate([state, jnp.zeros((AUG - HEAD_SIZE, AUG), f32)], axis=0).T
        grad_value = times(prepared(turn[:HEAD_SIZE]), feat)
        if f == len(wins) - 1:
            grad_key_ref[:, low:high] = grad_key
            grad_value_ref[:, low:high] = grad_value
        else:
            grad_key_ref[:, low:high] = jnp.where(keep, grad_key, grad_key_ref[:, low:high])
            grad_value_ref[:, low:high] = jnp.where(keep, grad_value, grad_value_ref[:, low:high])


def key_grads(key_feat, value_feat, later, part, after):
    tokens = key_feat.shape[1]
    heads, frames = part.shape[:2]
    wins = windows(frames, ROWS * COLS, tokens)
    block = pl.BlockSpec((HEAD_SIZE, tokens), lambda h: (h, 0))
    return pl.pallas_call(
        functools.partial(key_kernel, wins),
        grid=(heads,),
        in_specs=[
            block,
            block,
            pl.BlockSpec((1, HEAD_SIZE, AUG), lambda h: (h, 0, 0)),
            pl.BlockSpec((1, frames, HEAD_SIZE, AUG), lambda h: (h, 0, 0, 0)),
        ]
        + [pl.BlockSpec(memory_space=pltpu.HBM)] * len(after),
        out_specs=[block, block],
        out_shape=[in_hbm(key_feat.shape)] * 2,
        compiler_params=params(58),
        cost_estimate=cost(12 * heads * tokens * AUG * AUG, 16 * heads * HEAD_SIZE * tokens),
        name="key_grads",
    )(key_feat, value_feat, later, part, *after)


def topped_kernel(count, me_ref, *refs):
    for early_ref, halo_ref, out_ref in zip(refs, refs[count : 2 * count], refs[-count:]):
        out_ref[...] = early_ref[0] + halo_ref[0]


def topped(early, halo, after):
    count, steps = early.shape[:2]
    me = lax.axis_index("head").astype(jnp.int32).reshape(1)

    def block(s):
        return pl.BlockSpec((1, 1, *early.shape[2:]), lambda i, me: (me[0] ^ s, i, 0, 0))

    return pl.pallas_call(
        functools.partial(topped_kernel, count),
        grid_spec=pltpu.PrefetchScalarGridSpec(
            num_scalar_prefetch=1,
            grid=(steps,),
            in_specs=[block(s) for s in range(count)] * 2
            + [pl.BlockSpec(memory_space=pltpu.HBM)] * len(after),
            out_specs=[pl.BlockSpec((1, *early.shape[2:]), lambda i, me: (i, 0, 0))] * count,
        ),
        out_shape=[in_hbm((steps, *early.shape[2:]))] * count,
        compiler_params=params(58 if steps > 1 else 12),
        cost_estimate=cost(0, 0),
        name="topped",
    )(me, *[early] * count, *[halo] * count, *after)


def place_kernel(chans, count, *refs):
    late_ref, out_ref = refs[count], refs[-1]
    me = lax.axis_index("head")
    found = [ref[0] for ref in refs[:count]]
    bit = 1
    while bit < count:
        swap = (me & bit) != 0
        found = [jnp.where(swap, found[s ^ bit], found[s]) for s in range(count)]
        bit *= 2
    first = 0
    for blocks in (found, [late_ref[j, 0] for j in range(count)]):
        for k in range(blocks[0].shape[1] // chans):
            pieces = [block[:, k * chans : (k + 1) * chans] for block in blocks]
            out_ref[:, first, :] = jnp.concatenate(pieces, axis=1)
            first += 1


def placed(early, late, filled, start, steps, chans):
    count = len(early)
    rows = late.shape[2]
    frames = (early[0].shape[2] + late.shape[3]) // chans
    total = count * chans
    extra = [] if filled is None else [filled]
    blocks = [pl.BlockSpec((1, *a.shape[1:]), lambda i: (i, 0, 0)) for a in early]
    blocks.append(pl.BlockSpec((count, 1, *late.shape[2:]), lambda i: (0, i, 0, 0)))
    if steps == 1:
        blocks = [pl.BlockSpec(memory_space=pltpu.VMEM)] * (count + 1)
    return pl.pallas_call(
        functools.partial(place_kernel, chans, count),
        grid=(steps,),
        in_specs=blocks + [pl.BlockSpec(memory_space=pl.ANY)] * len(extra),
        out_specs=pl.BlockSpec((rows, frames, total), lambda i: (start + i, 0, 0)),
        out_shape=jax.ShapeDtypeStruct((rows * (ROWS // BLOCK), frames, total), f32),
        input_output_aliases={count + 1: 0} if extra else {},
        compiler_params=params(14 if steps == 1 else 28),
        cost_estimate=cost(0, 0),
        name="placed",
    )(*early, late, *extra)


def body(query_feat, key_feat, value_feat, grad_out, spatial_weight, temporal_weight):
    chans, tokens = query_feat.shape
    frames = tokens // (ROWS * COLS)
    heads = chans // HEAD_SIZE
    head_devs = lax.axis_size("head")
    segs = lax.axis_size("seg")
    local, totals = local_states(key_feat, value_feat, frames, heads)
    feat = turned(query_feat)
    parts = entering(totals, False, [feat])

    def sent(a):
        return lax.all_to_all(a, "head", split_axis=0, concat_axis=0, tiled=True)

    spans = [(0, 1), (1, ROWS // BLOCK - 1)]
    late, acts, after = [], [], []
    for start, steps in spans:
        a, act, weights = forward(
            parts, local, (spatial_weight, temporal_weight), feat, start, steps, head_devs, after
        )
        late.append(sent(a))
        acts.append(act)
        after = [act]
    shares = [first_frames(act, weights, chans, head_devs) for act in acts]
    pairs = [(i, i + 1) for i in range(segs - 1)]
    moved = [lax.ppermute(halo, "seg", pairs) for _, halo in shares]

    before = whole_state(parts, False)
    after = [late[0], shares[0][1], shares[1][1]]
    grad_query, part, back = query_grads(query_feat, grad_out, before, local, after)
    later = whole_state(entering(back, True, []), True)
    grad_key, grad_value = key_grads(key_feat, value_feat, later, part, [])

    def exchanged(blocks):
        moved = {s: xor_move(blocks[s], "head", s) for s in range(len(blocks) - 1, 0, -1)}
        return [blocks[0]] + [moved[s] for s in range(1, len(blocks))]

    ties = [[grad_key], [grad_query]]
    arrived = [
        exchanged(topped(early, halo, tie)) for (early, _), halo, tie in zip(shares, moved, ties)
    ]
    mixed = None
    for i in (1, 0):
        mixed = placed(arrived[i], late[i], mixed, *spans[i], chans)
    mixed = mixed.reshape(ROWS, COLS // head_devs, *mixed.shape[1:])
    return grad_query, grad_key, grad_value, jnp.transpose(mixed, (2, 0, 1, 3))


def solution(mesh):
    in_specs = (P("head", "seg"), P("head", "seg"), P("head", "seg"), P("head", "seg"), P(), P())
    out_specs = (P("head", "seg"), P("head", "seg"), P("head", "seg"), P("seg", None, "head", None))
    return jax.shard_map(body, mesh=mesh, in_specs=in_specs, out_specs=out_specs, check_vma=False)
```
